32 devices in a mesh: row: 8 (over z, y), col: 4 (over x, core).
Axes of the slice: x: 2, y: 2, z: 4, core: 2. Of those that a mesh axis runs over, the one named last changes fastest.
Arguments:
- image: bfloat16 [256, 128, 192], P('row', 'col'), may hold values from -6 to 6
- conv_weight: bfloat16 [3, 3, 192, 384], replicated, may hold values from -0.15625 to 0.15625
- conv_bias: float32 [384], replicated, may hold values from -3 to 3
- merge_gain: float32 [384], replicated, may hold values from 0.25 to 1.75
- merge_shift: float32 [384], replicated, may hold values from -3 to 3
- norm_gain: float32 [384], replicated, may hold values from 0.25 to 1.75
- norm_shift: float32 [384], replicated, may hold values from -3 to 3
- qkv_weight: bfloat16 [384, 1152], replicated, may hold values from -4 to 4
- proj_weight: bfloat16 [384, 384], replicated, may hold values from -0.3125 to 0.3125
- proj_bias: float32 [384], replicated, may hold values from -3 to 3
Outputs:
- block_out: bfloat16 [128, 64, 384], P('row', 'col')
The draws below stay inside these ranges and needn't reach their ends.
All inputs are finite; a program needn't handle non-finite values.
Results may differ from the reference program's by a relative error of at most 0.02.
The reference program's roundings to bfloat16 on the way (of `tokens`, `normed`, `qkv`, `probs` and `attention`) count: a program that leaves them out, or rounds other values in their place, can miss the bound.
Values may be sent and summed in bfloat16 or wider, within the bound.
No kernel may reach another device: no remote copies, remote signals or barrier semaphores. Data moves between devices by JAX's collectives and lax.ppermute only.
A program may use at most 128 MiB of HBM per device.

```python
import math
import jax
import jax.numpy as jnp
from jax import lax

IN_CH = 192
DIM = 384
HEADS = 16
SPLIT = 8
ROWS = 128
COLS = 64


def draw_qkv_weight(key, part):
    first, second = jax.random.split(key, 2)
    base = jax.random.truncated_normal(first, -3.0, 3.0, (DIM, 3 * DIM), jnp.float32)
    head_scale = jnp.exp(jax.random.uniform(second, (HEADS,), jnp.float32, math.log(1.2), math.log(2.2)))
    per_column = jnp.repeat(head_scale, DIM // HEADS)
    column_scale = jnp.concatenate([per_column, per_column, jnp.ones((DIM,), jnp.float32)])
    return (base * column_scale[None, :] / math.sqrt(DIM)).astype(jnp.bfloat16)


def shard_levels(stream_key, shape, pieces, least, top_value):
    level = 1.0
    for dim, shards_of in pieces:
        steps = jax.random.uniform(jax.random.fold_in(jax.random.fold_in(stream_key, 6), dim), (shards_of,), jnp.float32, least / len(pieces), top_value / len(pieces))
        level = level * jnp.repeat(jnp.exp(steps), shape[dim] // shards_of).reshape((-1,) + (1,) * (len(shape) - 1 - dim))
    return level


def normal_values(own_key, shape, scale, most, shards=(), held_as=jnp.bfloat16):
    entries = scale * jax.random.normal(own_key, shape, jnp.float32)
    if shards:
        entries = entries * shard_levels(own_key, shape, shards, -0.22, 0.18)
    return jnp.clip(entries, -most, most).astype(held_as)


def setup_inputs(seed: int = 0) -> dict:
    keys = jax.random.split(jax.random.key(seed), 11)
    image = normal_values(keys[0], (2 * ROWS, 2 * COLS, IN_CH), 1.0, 6.0, ((0, 8), (1, 4)))
    conv_weight = normal_values(keys[1], (3, 3, IN_CH, DIM), (9 * IN_CH) ** -0.5, 0.15625)
    conv_bias = normal_values(keys[2], (DIM,), 0.5, 3.0, (), jnp.float32)
    merge_gain = jnp.clip(1.0 + 0.15 * jax.random.normal(keys[3], (DIM,), jnp.float32), 0.25, 1.75)
    merge_shift = normal_values(keys[4], (DIM,), 0.5, 3.0, (), jnp.float32)
    norm_gain = jnp.clip(1.0 + 0.15 * jax.random.normal(keys[5], (DIM,), jnp.float32), 0.25, 1.75)
    norm_shift = normal_values(keys[6], (DIM,), 0.5, 3.0, (), jnp.float32)
    qkv_weight = draw_qkv_weight(jax.random.fold_in(keys[10], 71), 0)
    proj_weight = normal_values(keys[8], (DIM, DIM), DIM ** -0.5, 0.3125)
    proj_bias = normal_values(keys[9], (DIM,), 0.5, 3.0, (), jnp.float32)
    return {"image": image, "conv_weight": conv_weight, "conv_bias": conv_bias, "merge_gain": merge_gain, "merge_shift": merge_shift, "norm_gain": norm_gain, "norm_shift": norm_shift, "qkv_weight": qkv_weight, "proj_weight": proj_weight, "proj_bias": proj_bias}


def layer_norm(values, gain, shift):
    center = values - lax.optimization_barrier(jnp.mean(values, -1, keepdims=True))
    spread = lax.optimization_barrier(jnp.mean(center * center, -1, keepdims=True))
    return center * lax.rsqrt(spread + 1e-05) * gain + shift

def stripe_attention(block):
    wide = block.astype(jnp.float32)
    queries = wide[:, 0].transpose(1, 0, 2)
    key_rows = wide[:, 1].transpose(1, 0, 2)
    value_rows = wide[:, 2].transpose(1, 0, 2)
    scores = jnp.einsum('hqd,hkd->hqk', queries, key_rows) / math.sqrt(queries.shape[-1])
    highest = lax.optimization_barrier(jnp.max(scores, -1, keepdims=True))
    weights = jnp.exp(scores - highest)
    totals = lax.optimization_barrier(jnp.sum(weights, -1, keepdims=True))
    probs = lax.optimization_barrier(weights.astype(jnp.bfloat16)).astype(jnp.float32)
    mixed = jnp.einsum('hqk,hkd->hqd', probs, value_rows)
    return (mixed / totals).astype(jnp.bfloat16).transpose(1, 0, 2)

def reference(image, conv_weight, conv_bias, merge_gain, merge_shift, norm_gain, norm_shift, qkv_weight, proj_weight, proj_bias):
    heads_half = HEADS // 2
    depth = DIM // HEADS
    merged = lax.conv_general_dilated(image.astype(jnp.float32)[None], conv_weight.astype(jnp.float32), (2, 2), ((1, 0), (1, 0)), dimension_numbers=('NHWC', 'HWIO', 'NHWC'), precision=lax.Precision.HIGHEST)[0]
    merged = merged + conv_bias
    tokens = layer_norm(merged, merge_gain, merge_shift).astype(jnp.bfloat16)
    normed = layer_norm(tokens.astype(jnp.float32), norm_gain, norm_shift).astype(jnp.bfloat16)
    qkv = jnp.dot(normed.reshape(ROWS * COLS, DIM), qkv_weight, preferred_element_type=jnp.float32)
    qkv = qkv.astype(jnp.bfloat16).reshape(ROWS, COLS, 3, 2, heads_half, depth)
    row_blocks = qkv[:, :, :, 0].reshape(ROWS // SPLIT, SPLIT * COLS, 3, heads_half, depth)
    row_out = lax.map(stripe_attention, row_blocks).reshape(ROWS, COLS, heads_half, depth)
    col_blocks = qkv[:, :, :, 1].reshape(ROWS, COLS // SPLIT, SPLIT, 3, heads_half, depth)
    col_blocks = col_blocks.transpose(1, 0, 2, 3, 4, 5).reshape(COLS // SPLIT, ROWS * SPLIT, 3, heads_half, depth)
    col_out = lax.map(stripe_attention, col_blocks).reshape(COLS // SPLIT, ROWS, SPLIT, heads_half, depth)
    col_out = col_out.transpose(1, 0, 2, 3, 4).reshape(ROWS, COLS, heads_half, depth)
    attention = jnp.concatenate([row_out, col_out], 2).reshape(ROWS * COLS, DIM)
    output = tokens.astype(jnp.float32).reshape(ROWS * COLS, DIM)
    output = output + jnp.dot(attention, proj_weight, preferred_element_type=jnp.float32) + proj_bias
    return output.astype(jnp.bfloat16).reshape(ROWS, COLS, DIM)
```

```python
import math

import jax
import jax.numpy as jnp
from jax import lax
from jax.experimental import pallas as pl
from jax.experimental.pallas import tpu as pltpu
from jax.sharding import PartitionSpec as P

HEADS = 16
SPLIT = 8
HALF = HEADS // 2
F32 = jnp.float32
BF16 = jnp.bfloat16
LANES = 128


def params():
    return pltpu.CompilerParams(vmem_limit_bytes=48 * 1024 * 1024)


def vmem(count):
    return [pl.BlockSpec(memory_space=pltpu.VMEM)] * count


def dot(left, right):
    return jnp.dot(left, right, preferred_element_type=F32)


def layer_norm(values, gain, shift):
    center = values - jnp.mean(values, -1, keepdims=True)
    spread = jnp.mean(center * center, -1, keepdims=True)
    return center * lax.rsqrt(spread + 1e-05) * gain + shift


def quadrants(rows, cols):
    return [(a, b) for a in range(rows // SPLIT) for b in range(cols // SPLIT)]


def merge_kernel(
    image, upper, left, corner, weight, bias, gain, shift, gain2, shift2, qkv, tokens, normed, chunks, pixels
):
    in_rows, in_cols, channels = image.shape
    rows, cols = in_rows // 2, in_cols // 2
    width = weight.shape[3]
    depth = width // HEADS
    first = SPLIT
    parts = [(k, k * LANES, min(LANES, channels - k * LANES)) for k in range(pixels.shape[0])]
    for part, start, size in parts:
        lanes = pl.ds(0, size)
        here = pl.ds(start, size)
        pixels[part, pl.ds(1, in_rows), pl.ds(first, in_cols), lanes] = image[:, :, here].astype(F32)
        pixels[part, 0, pl.ds(first, in_cols), lanes] = upper[0, :, here].astype(F32)
        pixels[part, 0, pl.ds(first - 1, 1), lanes] = corner[0, :, here].astype(F32)[in_cols - 1 :]
        beside = left[:, here].astype(F32)
        for i in range(in_rows):
            pixels[part, 1 + i, pl.ds(first - 1, 1), lanes] = beside[i : i + 1]
    merged = jnp.zeros((rows * cols, width), F32)
    for tap in range(3):
        pieces = []
        for part, start, size in parts:
            stack = [
                pixels[part, i, pl.ds(first - 1 + tap, cols, stride=2), :] for i in range(in_rows + 1)
            ]
            pieces.append((stack, size))
        for tap_row in range(3):
            window = jnp.concatenate(
                [
                    jnp.concatenate(stack[tap_row : tap_row + 2 * rows - 1 : 2], 0)[:, :size]
                    for stack, size in pieces
                ],
                1,
            ).astype(BF16)
            merged = merged + dot(window, weight[tap_row, tap])
    merged = (merged + bias[...]).reshape(rows, cols, width)
    merged = jnp.concatenate(
        [
            merged[a * SPLIT : (a + 1) * SPLIT, b * SPLIT : (b + 1) * SPLIT].reshape(SPLIT * SPLIT, width)
            for a, b in quadrants(rows, cols)
        ],
        0,
    )
    held = layer_norm(merged, gain[...], shift[...]).astype(BF16)
    tokens[...] = held
    again = layer_norm(held.astype(F32), gain2[...], shift2[...]).astype(BF16)
    normed[...] = again
    across = cols // SPLIT
    count = chunks.shape[0]
    per = across * HALF // count
    for b in range(across):
        mine = [
            again[(a * across + b) * SPLIT * SPLIT : (a * across + b + 1) * SPLIT * SPLIT]
            for a in range(rows // SPLIT)
        ]
        mine = jnp.concatenate(mine, 0)
        lines = []
        for kind in range(3):
            begin = kind * width + width // 2
            base = begin // LANES * LANES
            wide = dot(mine, qkv[:, base : (kind + 1) * width])
            lines.append(wide.T[begin - base :])
        for item in range(b * HALF, (b + 1) * HALF, per):
            low = (item - b * HALF) * depth
            chunks[item // per] = jnp.concatenate(
                [kind[low : low + per * depth] for kind in lines], 0
            ).astype(BF16)


def row_qkv_kernel(normed, qkv, queries, pairs):
    width = normed.shape[1]
    half = width // 2
    step = normed.shape[0] // queries.shape[0]
    for a in range(queries.shape[0]):
        mine = normed[a * step : (a + 1) * step]
        for kind in range(3):
            begin = kind * width
            end = begin + -(-half // LANES) * LANES
            lines = dot(mine, qkv[:, begin:end]).T[:half].astype(BF16)
            if kind == 0:
                queries[a] = lines
            else:
                pairs[a, (kind - 1) * half : kind * half] = lines


def padded_rows(values, start, total):
    size, lanes = values.shape
    pieces = []
    if start:
        pieces.append(jnp.zeros((start, lanes), F32))
    pieces.append(values)
    if total - start - size:
        pieces.append(jnp.zeros((total - start - size, lanes), F32))
    return jnp.concatenate(pieces, 0)


def with_sum_row(values):
    lanes = values.shape[1]
    return jnp.concatenate(
        [values, jnp.ones((1, lanes), F32), jnp.zeros((7, lanes), F32)], 0
    ).astype(BF16)


def weights_of(scores, depth):
    highest = jnp.max(scores, 0, keepdims=True)
    return jnp.exp2((scores - highest) * (math.log2(math.e) / math.sqrt(depth))).astype(BF16)


def col_attention_kernel(depth, arrived, result):
    count, lines, length = arrived.shape
    per = lines // (3 * depth)
    total = per * depth
    lanes = jnp.concatenate([arrived[s].astype(F32) for s in range(count)], 1)
    key_rows = lanes[total : 2 * total].T.astype(BF16)
    block = 2 * length
    outs = []
    for begin in range(0, count * length, block):
        heads = []
        for h in range(per):
            queries = padded_rows(lanes[h * depth : (h + 1) * depth, begin : begin + block], h * depth, total)
            scores = dot(key_rows, queries.astype(BF16))
            probs = weights_of(scores, depth)
            values = with_sum_row(lanes[2 * total + h * depth : 2 * total + (h + 1) * depth])
            mixed = dot(values, probs)
            heads.append(mixed[:depth] / mixed[depth : depth + 1])
        heads = jnp.concatenate(heads, 0).astype(BF16)
        for k in range(block // length):
            result[begin // length + k] = heads[:, k * length : (k + 1) * length]


def row_attention_kernel(count, queries, *refs):
    pairs = refs[:count]
    tokens, weight, bias, partial = refs[count:]
    stripes, half, length = queries.shape
    depth = half // HALF
    for a in range(stripes):
        both = jnp.concatenate([ref[a].astype(F32) for ref in pairs], 1)
        key_rows = both[:half].T.astype(BF16)
        lines = queries[a].astype(F32)
        heads = []
        for h in range(0, HALF, 2):
            wide = jnp.concatenate(
                [
                    padded_rows(lines[g * depth : (g + 1) * depth], g * depth, half)
                    for g in (h, h + 1)
                ],
                1,
            ).astype(BF16)
            probs = weights_of(dot(key_rows, wide), depth)
            for k, g in enumerate((h, h + 1)):
                values = with_sum_row(both[half + g * depth : half + (g + 1) * depth])
                mixed = dot(values, probs[:, k * length : (k + 1) * length])
                heads.append(mixed[:depth] / mixed[depth : depth + 1])
        attention = jnp.concatenate(heads, 0).T.astype(BF16)
        here = pl.ds(a * length, length)
        partial[here] = tokens[here].astype(F32) + dot(attention, weight[:half]) + bias[...]


def output_kernel(arrived, partial, weight, output):
    rows, cols, width = output.shape
    half = width // 2
    count = arrived.shape[0]
    across = cols // SPLIT
    down = rows // SPLIT
    square = SPLIT * SPLIT
    each = count // across
    blocks = {}
    for b in range(across):
        lines = jnp.concatenate([arrived[b * each + k].astype(F32) for k in range(each)], 0)
        mixed = dot(lines.T.astype(BF16), weight[half:])
        for a in range(down):
            here = pl.ds((a * across + b) * square, square)
            blocks[a, b] = (partial[here] + mixed[a * square : (a + 1) * square]).reshape(
                SPLIT, SPLIT, width
            )
    for a in range(down):
        output[a * SPLIT : (a + 1) * SPLIT] = jnp.concatenate(
            [blocks[a, b] for b in range(across)], 1
        ).astype(BF16)


def call(kernel, name, out_shape, args, flops, scratch=()):
    moved = sum(x.size * x.dtype.itemsize for x in args)
    return pl.pallas_call(
        kernel,
        out_shape=out_shape,
        in_specs=vmem(len(args)),
        out_specs=jax.tree.map(lambda _: pl.BlockSpec(memory_space=pltpu.VMEM), out_shape),
        scratch_shapes=scratch,
        compiler_params=params(),
        cost_estimate=pl.CostEstimate(flops=flops, bytes_accessed=moved, transcendentals=0),
        name=name,
    )(*args)


def shape(dims, dtype=BF16):
    return jax.ShapeDtypeStruct(dims, dtype)


def gathered(value, axis):
    held = [value]
    bit = lax.axis_size(axis) // 2
    while bit:
        pairs = [(k, k ^ bit) for k in range(lax.axis_size(axis))]
        held = held + [lax.ppermute(block, axis, pairs) for block in held]
        bit //= 2
    return held


def on_device(
    image,
    conv_weight,
    conv_bias,
    merge_gain,
    merge_shift,
    norm_gain,
    norm_shift,
    qkv_weight,
    proj_weight,
    proj_bias,
):
    in_rows, in_cols, channels = image.shape
    rows, cols = in_rows // 2, in_cols // 2
    width = conv_weight.shape[3]
    half = width // 2
    depth = width // HEADS
    row_count = lax.axis_size("row")
    col_count = lax.axis_size("col")
    down = [(k, k + 1) for k in range(row_count - 1)]
    right = [(k, k + 1) for k in range(col_count - 1)]
    upper = lax.ppermute(image[-1:], "row", down)
    left = lax.ppermute(image[:, -1], "col", right)
    corner = lax.ppermute(upper, "col", right)
    row = lambda value: value.reshape(1, width)
    stripes, across = rows // SPLIT, cols // SPLIT
    per = across * HALF // row_count
    lanes = rows * SPLIT
    tokens, normed, chunks = call(
        merge_kernel,
        "merge",
        (
            shape((rows * cols, width)),
            shape((rows * cols, width)),
            shape((row_count, 3 * per * depth, lanes)),
        ),
        (
            image,
            upper,
            left,
            corner,
            conv_weight,
            row(conv_bias),
            row(merge_gain),
            row(merge_shift),
            row(norm_gain),
            row(norm_shift),
            qkv_weight,
        ),
        10**9,
        [pltpu.VMEM((-(-channels // LANES), in_rows + 1, in_cols + SPLIT, LANES), F32)],
    )
    arrived = lax.all_to_all(chunks, "row", 0, 0, tiled=True)
    queries, pairs = call(
        row_qkv_kernel,
        "row_qkv",
        (shape((stripes, half, cols * SPLIT)), shape((stripes, width, cols * SPLIT))),
        (normed, qkv_weight),
        3 * 10**8,
    )
    held = gathered(pairs, "col")
    result = call(
        lambda *refs: col_attention_kernel(depth, *refs),
        "col_attention",
        shape((row_count, per * depth, lanes)),
        (arrived,),
        2 * 10**9,
    )
    back = lax.all_to_all(result, "row", 0, 0, tiled=True)
    partial = call(
        lambda *refs: row_attention_kernel(len(held), *refs),
        "row_attention",
        shape((rows * cols, width), F32),
        (queries, *held, tokens, proj_weight, row(proj_bias)),
        2 * 10**9,
    )
    return call(
        output_kernel,
        "output",
        shape((rows, cols, width)),
        (back, partial, proj_weight),
        10**8,
    )


def solution(mesh):
    return jax.shard_map(
        on_device,
        mesh=mesh,
        in_specs=(P("row", "col", None), P(), P(), P(), P(), P(), P(), P(), P(), P()),
        out_specs=P("row", "col", None),
        check_vma=False,
    )
```

```python
import math

import jax
import jax.numpy as jnp
from jax import lax
from jax.experimental import pallas as pl
from jax.experimental.pallas import tpu as pltpu
from jax.sharding import PartitionSpec as P

HEADS = 16
SPLIT = 8
HALF = HEADS // 2
F32 = jnp.float32
BF16 = jnp.bfloat16
LANES = 128


def params():
    return pltpu.CompilerParams(vmem_limit_bytes=48 * 1024 * 1024)


def vmem(count):
    return [pl.BlockSpec(memory_space=pltpu.VMEM)] * count


def dot(left, right):
    return jnp.dot(left, right, preferred_element_type=F32)


def layer_norm(values, gain, shift):
    center = values - jnp.mean(values, -1, keepdims=True)
    spread = jnp.mean(center * center, -1, keepdims=True)
    return center * lax.rsqrt(spread + 1e-05) * gain + shift


def quadrants(rows, cols):
    return [(a, b) for a in range(rows // SPLIT) for b in range(cols // SPLIT)]


def lane_parts(channels):
    return [(k, k * LANES, min(LANES, channels - k * LANES)) for k in range(-(-channels // LANES))]


def every_second(ref, index, first, count, channels):
    return jnp.concatenate(
        [ref[(part, *index, pl.ds(first, count, stride=2))][:, :size] for part, _, size in lane_parts(channels)],
        1,
    )


def edge_kernel(image, bottom, side):
    rows, cols, _ = image.shape
    bottom[...] = image[rows - 1 :]
    side[...] = image[:, cols - 2 * SPLIT :].astype(F32)[:, 2 * SPLIT - 1].astype(BF16)


def join_kernel(side, upper, joined):
    size = side.shape[0]
    extra = joined.shape[0] - size
    joined[:size] = side[...]
    joined[size:] = upper[0, upper.shape[1] - extra :]


def own_kernel(image, weight, merged, pixels):
    in_rows, in_cols, channels = image.shape
    rows, cols = in_rows // 2, in_cols // 2
    first = SPLIT
    pixels[:, 0] = jnp.zeros(pixels.shape[:1] + pixels.shape[2:], F32)
    pixels[:, :, :first] = jnp.zeros(pixels.shape[:2] + (first, LANES), F32)
    for part, start, size in lane_parts(channels):
        pixels[part, pl.ds(1, in_rows), pl.ds(first, in_cols), pl.ds(0, size)] = image[
            :, :, pl.ds(start, size)
        ].astype(F32)
    total = jnp.zeros((rows * cols, merged.shape[1]), F32)
    for tap in range(3):
        lines = [
            every_second(pixels, (i,), first - 1 + tap, cols, channels).astype(BF16)
            for i in range(in_rows + 1)
        ]
        for tap_row in range(3):
            window = jnp.concatenate(lines[tap_row : tap_row + 2 * rows - 1 : 2], 0)
            total = total + dot(window, weight[tap_row, tap])
    merged[...] = total


def merge_kernel(
    merged, upper, joined, weight, qkv, bias, gain, shift, gain2, shift2, tokens, normed, chunks, edges
):
    in_cols, channels = upper.shape[1:]
    in_rows = 2 * merged.shape[0] // (in_cols // 2)
    rows, cols = in_rows // 2, in_cols // 2
    width = weight.shape[3]
    depth = width // HEADS
    first = SPLIT
    row = lambda ref: ref[...].reshape(1, width)
    for part, start, size in lane_parts(channels):
        lanes, here = pl.ds(0, size), pl.ds(start, size)
        beside = joined[:, here].astype(F32)
        edges[part, 0, pl.ds(first, in_cols), lanes] = upper[0, :, here].astype(F32)
        edges[part, 0, pl.ds(first - 1, 1), lanes] = beside[beside.shape[0] - 1 :]
        edges[part, 1, pl.ds(first, in_rows), lanes] = beside[:in_rows]
        edges[part, 1, pl.ds(first - 1, 1), lanes] = jnp.zeros((1, size), F32)
    above = [every_second(edges, (0,), first - 1 + tap, cols, channels).astype(BF16) for tap in range(3)]
    aside = [every_second(edges, (1,), first - 1 + tap, rows, channels).astype(BF16) for tap in range(3)]
    corner = dot(jnp.concatenate([above[0], aside[0]], 0), weight[0, 0])
    top = corner[:cols] + dot(above[1], weight[0, 1]) + dot(above[2], weight[0, 2])
    near = corner[cols:] + dot(aside[1], weight[1, 0]) + dot(aside[2], weight[2, 0])
    grid = merged[...].reshape(rows, cols, width)
    grid = jnp.concatenate([grid[:1] + top.reshape(1, cols, width), grid[1:]], 0)
    begin = lax.broadcasted_iota(jnp.int32, (rows, SPLIT, width), 1) == 0
    grid = jnp.concatenate(
        [grid[:, :SPLIT] + jnp.where(begin, near.reshape(rows, 1, width), 0.0), grid[:, SPLIT:]], 1
    )
    grid = jnp.concatenate(
        [
            grid[a * SPLIT : (a + 1) * SPLIT, b * SPLIT : (b + 1) * SPLIT].reshape(SPLIT * SPLIT, width)
            for a, b in quadrants(rows, cols)
        ],
        0,
    )
    held = layer_norm(grid + row(bias), row(gain), row(shift)).astype(BF16)
    tokens[...] = held
    again = layer_norm(held.astype(F32), row(gain2), row(shift2)).astype(BF16)
    normed[...] = again
    across = cols // SPLIT
    count = chunks.shape[0]
    per = across * HALF // count
    square = SPLIT * SPLIT
    for b in range(across):
        mine = [
            again[(a * across + b) * square : (a * across + b + 1) * square] for a in range(rows // SPLIT)
        ]
        mine = jnp.concatenate(mine, 0)
        lines = []
        for kind in range(3):
            begin = kind * width + width // 2
            base = begin // LANES * LANES
            wide = dot(mine, qkv[:, base : (kind + 1) * width])
            lines.append(wide.T[begin - base :])
        for item in range(b * HALF, (b + 1) * HALF, per):
            low = (item - b * HALF) * depth
            chunks[item // per] = jnp.concatenate(
                [kind[low : low + per * depth] for kind in lines], 0
            ).astype(BF16)


def row_qkv_kernel(normed, qkv, queries, pairs):
    width = normed.shape[1]
    half = width // 2
    step = normed.shape[0] // queries.shape[0]
    for a in range(queries.shape[0]):
        mine = normed[a * step : (a + 1) * step]
        for kind in range(3):
            begin = kind * width
            end = begin + -(-half // LANES) * LANES
            lines = dot(mine, qkv[:, begin:end]).T[:half].astype(BF16)
            if kind == 0:
                queries[a] = lines
            else:
                pairs[a, (kind - 1) * half : kind * half] = lines


def padded_rows(values, start, total):
    size, lanes = values.shape
    pieces = []
    if start:
        pieces.append(jnp.zeros((start, lanes), F32))
    pieces.append(values)
    if total - start - size:
        pieces.append(jnp.zeros((total - start - size, lanes), F32))
    return jnp.concatenate(pieces, 0)


def with_sum_row(values):
    lanes = values.shape[1]
    return jnp.concatenate(
        [values, jnp.ones((1, lanes), F32), jnp.zeros((7, lanes), F32)], 0
    ).astype(BF16)


def weights_of(scores, highest, depth):
    return jnp.exp2((scores - highest) * (math.log2(math.e) / math.sqrt(depth))).astype(BF16)


def ahead_of(items, score, finish, ahead):
    waiting = [score(item) for item in items[:ahead]]
    for k, item in enumerate(items):
        if k + ahead < len(items):
            waiting.append(score(items[k + ahead]))
        finish(item, *waiting.pop(0))


def attended(mixed, depth):
    return mixed[:depth] / mixed[depth : depth + 1]


def col_attention_kernel(depth, arrived, result):
    count, lines, length = arrived.shape
    per = lines // (3 * depth)
    total = per * depth
    lanes = jnp.concatenate([arrived[s].astype(F32) for s in range(count)], 1)
    key_rows = lanes[total : 2 * total].T.astype(BF16)
    values = [
        with_sum_row(lanes[2 * total + h * depth : 2 * total + (h + 1) * depth]) for h in range(per)
    ]
    block = 4 * length
    done = {}

    def score(item):
        begin, h = item
        queries = padded_rows(lanes[h * depth : (h + 1) * depth, begin : begin + block], h * depth, total)
        scores = dot(key_rows, queries.astype(BF16))
        return scores, jnp.max(scores, 0, keepdims=True)

    def finish(item, scores, highest):
        done[item] = attended(dot(values[item[1]], weights_of(scores, highest, depth)), depth)

    starts = range(0, count * length, block)
    ahead_of([(begin, h) for begin in starts for h in range(per)], score, finish, 1)
    for begin in starts:
        heads = jnp.concatenate([done[begin, h] for h in range(per)], 0).astype(BF16)
        for k in range(block // length):
            result[begin // length + k] = heads[:, k * length : (k + 1) * length]


def row_attention_kernel(count, queries, *refs):
    pairs = refs[:count]
    tokens, weight, bias, partial = refs[count:]
    stripes, half, length = queries.shape
    depth = half // HALF
    together = 2
    both, key_rows, lines, done = [], [], [], {}
    for a in range(stripes):
        both.append(jnp.concatenate([ref[a].astype(F32) for ref in pairs], 1))
        key_rows.append(both[a][:half].T.astype(BF16))
        lines.append(queries[a].astype(F32))

    def score(item):
        a, h = item
        wide = [
            padded_rows(lines[a][g * depth : (g + 1) * depth], g * depth, half)
            for g in range(h, h + together)
        ]
        scores = dot(key_rows[a], jnp.concatenate(wide, 1).astype(BF16))
        return scores, jnp.max(scores, 0, keepdims=True)

    def finish(item, scores, highest):
        a, h = item
        probs = weights_of(scores, highest, depth)
        for k in range(together):
            g = h + k
            values = with_sum_row(both[a][half + g * depth : half + (g + 1) * depth])
            done[a, g] = attended(dot(values, probs[:, k * length : (k + 1) * length]), depth)

    items = [(a, h) for a in range(stripes) for h in range(0, HALF, together)]
    ahead_of(items, score, finish, 2)
    for a in range(stripes):
        attention = jnp.concatenate([done[a, g] for g in range(HALF)], 0).T.astype(BF16)
        here = pl.ds(a * length, length)
        partial[here] = (
            tokens[here].astype(F32) + dot(attention, weight[:half]) + bias[...].reshape(1, 2 * half)
        )


def output_kernel(arrived, partial, weight, output):
    rows, cols, width = output.shape
    half = width // 2
    count = arrived.shape[0]
    across = cols // SPLIT
    down = rows // SPLIT
    square = SPLIT * SPLIT
    each = count // across
    blocks = {}
    for b in range(across):
        lines = jnp.concatenate([arrived[b * each + k].astype(F32) for k in range(each)], 0)
        mixed = dot(lines.T.astype(BF16), weight[half:])
        for a in range(down):
            here = pl.ds((a * across + b) * square, square)
            blocks[a, b] = (partial[here] + mixed[a * square : (a + 1) * square]).reshape(
                SPLIT, SPLIT, width
            )
    for a in range(down):
        output[a * SPLIT : (a + 1) * SPLIT] = jnp.concatenate(
            [blocks[a, b] for b in range(across)], 1
        ).astype(BF16)


def call(kernel, name, out_shape, args, flops, scratch=()):
    moved = sum(x.size * x.dtype.itemsize for x in args)
    return pl.pallas_call(
        kernel,
        out_shape=out_shape,
        in_specs=vmem(len(args)),
        out_specs=jax.tree.map(lambda _: pl.BlockSpec(memory_space=pltpu.VMEM), out_shape),
        scratch_shapes=scratch,
        compiler_params=params(),
        cost_estimate=pl.CostEstimate(flops=flops, bytes_accessed=moved, transcendentals=0),
        name=name,
    )(*args)


def shape(dims, dtype=BF16):
    return jax.ShapeDtypeStruct(dims, dtype)


def gathered(value, axis):
    held = [value]
    bit = lax.axis_size(axis) // 2
    while bit:
        pairs = [(k, k ^ bit) for k in range(lax.axis_size(axis))]
        held = held + [lax.ppermute(block, axis, pairs) for block in held]
        bit //= 2
    return held


def on_device(
    image,
    conv_weight,
    conv_bias,
    merge_gain,
    merge_shift,
    norm_gain,
    norm_shift,
    qkv_weight,
    proj_weight,
    proj_bias,
):
    in_rows, in_cols, channels = image.shape
    rows, cols = in_rows // 2, in_cols // 2
    width = conv_weight.shape[3]
    half = width // 2
    depth = width // HEADS
    row_count = lax.axis_size("row")
    col_count = lax.axis_size("col")
    down = [(k, k + 1) for k in range(row_count - 1)]
    right = [(k, k + 1) for k in range(col_count - 1)]
    near = 2 * SPLIT
    bottom, side = call(
        edge_kernel,
        "edge",
        (shape((1, in_cols, channels)), shape((in_rows, channels))),
        (image,),
        10**10,
    )
    upper = lax.ppermute(bottom, "row", down)
    pixel_parts = -(-channels // LANES)
    merged = call(
        own_kernel,
        "own_tile",
        shape((rows * cols, width), F32),
        (image, conv_weight),
        10**9,
        [pltpu.VMEM((pixel_parts, in_rows + 1, in_cols + SPLIT, LANES), F32)],
    )
    joined = call(
        join_kernel, "join", shape((in_rows + near, channels)), (side, upper), 10**5
    )
    joined = lax.ppermute(joined, "col", right)
    stripes, across = rows // SPLIT, cols // SPLIT
    per = across * HALF // row_count
    lanes = rows * SPLIT
    tokens, normed, chunks = call(
        merge_kernel,
        "merge",
        (
            shape((rows * cols, width)),
            shape((rows * cols, width)),
            shape((row_count, 3 * per * depth, lanes)),
        ),
        (
            merged,
            upper,
            joined,
            conv_weight,
            qkv_weight,
            conv_bias,
            merge_gain,
            merge_shift,
            norm_gain,
            norm_shift,
        ),
        5 * 10**8,
        [pltpu.VMEM((pixel_parts, 2, max(in_rows, in_cols) + SPLIT, LANES), F32)],
    )
    arrived = lax.all_to_all(chunks, "row", 0, 0, tiled=True)
    queries, pairs = call(
        row_qkv_kernel,
        "row_qkv",
        (shape((stripes, half, cols * SPLIT)), shape((stripes, width, cols * SPLIT))),
        (normed, qkv_weight),
        3 * 10**8,
    )
    held = gathered(pairs, "col")
    result = call(
        lambda *refs: col_attention_kernel(depth, *refs),
        "col_attention",
        shape((row_count, per * depth, lanes)),
        (arrived,),
        2 * 10**9,
    )
    back = lax.all_to_all(result, "row", 0, 0, tiled=True)
    partial = call(
        lambda *refs: row_attention_kernel(len(held), *refs),
        "row_attention",
        shape((rows * cols, width), F32),
        (queries, *held, tokens, proj_weight, proj_bias),
        2 * 10**9,
    )
    return call(
        output_kernel,
        "output",
        shape((rows, cols, width)),
        (back, partial, proj_weight),
        10**8,
    )


def solution(mesh):
    return jax.shard_map(
        on_device,
        mesh=mesh,
        in_specs=(P("row", "col", None), P(), P(), P(), P(), P(), P(), P(), P(), P()),
        out_specs=P("row", "col", None),
        check_vma=False,
    )
```

```python
import math

import jax
import jax.numpy as jnp
from jax import lax
from jax.experimental import pallas as pl
from jax.experimental.pallas import tpu as pltpu
from jax.sharding import PartitionSpec as P

HEADS = 16
SPLIT = 8
HALF = HEADS // 2
F32 = jnp.float32
BF16 = jnp.bfloat16
LANES = 128


def params():
    return pltpu.CompilerParams(vmem_limit_bytes=48 * 1024 * 1024)


def vmem(count):
    return [pl.BlockSpec(memory_space=pltpu.VMEM)] * count


def dot(left, right):
    return jnp.dot(left, right, preferred_element_type=F32)


def layer_norm(values, gain, shift):
    center = values - jnp.mean(values, -1, keepdims=True)
    spread = jnp.mean(center * center, -1, keepdims=True)
    return center * lax.rsqrt(spread + 1e-05) * gain + shift


def quadrants(rows, cols):
    return [(a, b) for a in range(rows // SPLIT) for b in range(cols // SPLIT)]


def lane_parts(channels):
    return [(k, k * LANES, min(LANES, channels - k * LANES)) for k in range(-(-channels // LANES))]


def every_second(ref, index, first, count, channels):
    return jnp.concatenate(
        [ref[(part, *index, pl.ds(first, count, stride=2))][:, :size] for part, _, size in lane_parts(channels)],
        1,
    )


def edge_kernel(image, bottom, side):
    rows, cols, _ = image.shape
    bottom[...] = image[rows - 1 :]
    side[...] = image[:, cols - 2 * SPLIT :].astype(F32)[:, 2 * SPLIT - 1].astype(BF16)


def join_kernel(side, upper, joined):
    size = side.shape[0]
    extra = joined.shape[0] - size
    joined[:size] = side[...]
    joined[size:] = upper[0, upper.shape[1] - extra :]


def own_kernel(image, weight, merged, pixels):
    in_rows, in_cols, channels = image.shape
    rows, cols = in_rows // 2, in_cols // 2
    first = SPLIT
    pixels[:, 0] = jnp.zeros(pixels.shape[:1] + pixels.shape[2:], F32)
    pixels[:, :, :first] = jnp.zeros(pixels.shape[:2] + (first, LANES), F32)
    for part, start, size in lane_parts(channels):
        pixels[part, pl.ds(1, in_rows), pl.ds(first, in_cols), pl.ds(0, size)] = image[
            :, :, pl.ds(start, size)
        ].astype(F32)
    total = jnp.zeros((rows * cols, merged.shape[1]), F32)
    for tap in range(3):
        lines = [
            every_second(pixels, (i,), first - 1 + tap, cols, channels).astype(BF16)
            for i in range(in_rows + 1)
        ]
        for tap_row in range(3):
            window = jnp.concatenate(lines[tap_row : tap_row + 2 * rows - 1 : 2], 0)
            total = total + dot(window, weight[tap_row, tap])
    merged[...] = total


def merge_kernel(
    merged, upper, joined, weight, qkv, bias, gain, shift, gain2, shift2, tokens, normed, chunks, edges
):
    in_cols, channels = upper.shape[1:]
    in_rows = 2 * merged.shape[0] // (in_cols // 2)
    rows, cols = in_rows // 2, in_cols // 2
    width = weight.shape[3]
    depth = width // HEADS
    first = SPLIT
    row = lambda ref: ref[...].reshape(1, width)
    for part, start, size in lane_parts(channels):
        lanes, here = pl.ds(0, size), pl.ds(start, size)
        beside = joined[:, here].astype(F32)
        edges[part, 0, pl.ds(first, in_cols), lanes] = upper[0, :, here].astype(F32)
        edges[part, 0, pl.ds(first - 1, 1), lanes] = beside[beside.shape[0] - 1 :]
        edges[part, 1, pl.ds(first, in_rows), lanes] = beside[:in_rows]
        edges[part, 1, pl.ds(first - 1, 1), lanes] = jnp.zeros((1, size), F32)
    above = [every_second(edges, (0,), first - 1 + tap, cols, channels).astype(BF16) for tap in range(3)]
    aside = [every_second(edges, (1,), first - 1 + tap, rows, channels).astype(BF16) for tap in range(3)]
    corner = dot(jnp.concatenate([above[0], aside[0]], 0), weight[0, 0])
    top = corner[:cols] + dot(above[1], weight[0, 1]) + dot(above[2], weight[0, 2])
    near = corner[cols:] + dot(aside[1], weight[1, 0]) + dot(aside[2], weight[2, 0])
    grid = merged[...].reshape(rows, cols, width)
    grid = jnp.concatenate([grid[:1] + top.reshape(1, cols, width), grid[1:]], 0)
    begin = lax.broadcasted_iota(jnp.int32, (rows, SPLIT, width), 1) == 0
    grid = jnp.concatenate(
        [grid[:, :SPLIT] + jnp.where(begin, near.reshape(rows, 1, width), 0.0), grid[:, SPLIT:]], 1
    )
    grid = jnp.concatenate(
        [
            grid[a * SPLIT : (a + 1) * SPLIT, b * SPLIT : (b + 1) * SPLIT].reshape(SPLIT * SPLIT, width)
            for a, b in quadrants(rows, cols)
        ],
        0,
    )
    held = layer_norm(grid + row(bias), row(gain), row(shift)).astype(BF16)
    tokens[...] = held
    again = layer_norm(held.astype(F32), row(gain2), row(shift2)).astype(BF16)
    normed[...] = again
    across = cols // SPLIT
    count = chunks.shape[0]
    per = across * HALF // count
    square = SPLIT * SPLIT
    for b in range(across):
        mine = [
            again[(a * across + b) * square : (a * across + b + 1) * square] for a in range(rows // SPLIT)
        ]
        mine = jnp.concatenate(mine, 0)
        lines = []
        for kind in range(3):
            begin = kind * width + width // 2
            base = begin // LANES * LANES
            wide = dot(mine, qkv[:, base : (kind + 1) * width])
            lines.append(wide.T[begin - base :])
        for item in range(b * HALF, (b + 1) * HALF, per):
            low = (item - b * HALF) * depth
            chunks[item // per] = jnp.concatenate(
                [kind[low : low + per * depth] for kind in lines], 0
            ).astype(BF16)


def row_qkv_kernel(normed, qkv, queries, pairs):
    width = normed.shape[1]
    half = width // 2
    step = normed.shape[0] // queries.shape[0]
    for a in range(queries.shape[0]):
        mine = normed[a * step : (a + 1) * step]
        for kind in range(3):
            begin = kind * width
            end = begin + -(-half // LANES) * LANES
            lines = dot(mine, qkv[:, begin:end]).T[:half].astype(BF16)
            if kind == 0:
                queries[a] = lines
            else:
                pairs[a, (kind - 1) * half : kind * half] = lines


def padded_rows(values, start, total):
    size, lanes = values.shape
    pieces = []
    if start:
        pieces.append(jnp.zeros((start, lanes), F32))
    pieces.append(values)
    if total - start - size:
        pieces.append(jnp.zeros((total - start - size, lanes), F32))
    return jnp.concatenate(pieces, 0)


def with_sum_row(values):
    lanes = values.shape[1]
    return jnp.concatenate(
        [values, jnp.ones((1, lanes), F32), jnp.zeros((7, lanes), F32)], 0
    ).astype(BF16)


def weights_of(scores, highest, depth):
    return jnp.exp2((scores - highest) * (math.log2(math.e) / math.sqrt(depth))).astype(BF16)


def ahead_of(items, score, finish, ahead):
    waiting = [score(item) for item in items[:ahead]]
    for k, item in enumerate(items):
        if k + ahead < len(items):
            waiting.append(score(items[k + ahead]))
        finish(item, *waiting.pop(0))


def attended(mixed, depth):
    return mixed[:depth] / mixed[depth : depth + 1]


def col_attention_kernel(depth, arrived, result):
    count, lines, length = arrived.shape
    per = lines // (3 * depth)
    total = per * depth
    lanes = jnp.concatenate([arrived[s].astype(F32) for s in range(count)], 1)
    key_rows = lanes[total : 2 * total].T.astype(BF16)
    values = [
        with_sum_row(lanes[2 * total + h * depth : 2 * total + (h + 1) * depth]) for h in range(per)
    ]
    block = 4 * length
    done = {}

    def score(item):
        begin, h = item
        queries = padded_rows(lanes[h * depth : (h + 1) * depth, begin : begin + block], h * depth, total)
        scores = dot(key_rows, queries.astype(BF16))
        return scores, jnp.max(scores, 0, keepdims=True)

    def finish(item, scores, highest):
        done[item] = attended(dot(values[item[1]], weights_of(scores, highest, depth)), depth)

    starts = range(0, count * length, block)
    ahead_of([(begin, h) for begin in starts for h in range(per)], score, finish, 1)
    for begin in starts:
        heads = jnp.concatenate([done[begin, h] for h in range(per)], 0).astype(BF16)
        for k in range(block // length):
            result[begin // length + k] = heads[:, k * length : (k + 1) * length]


def row_attention_kernel(count, queries, *refs):
    pairs = refs[:count]
    tokens, weight, bias, partial = refs[count:]
    stripes, half, length = queries.shape
    depth = half // HALF
    together = 2
    both, key_rows, lines, done = [], [], [], {}
    for a in range(stripes):
        both.append(jnp.concatenate([ref[a].astype(F32) for ref in pairs], 1))
        key_rows.append(both[a][:half].T.astype(BF16))
        lines.append(queries[a].astype(F32))

    def score(item):
        a, h = item
        wide = [
            padded_rows(lines[a][g * depth : (g + 1) * depth], g * depth, half)
            for g in range(h, h + together)
        ]
        scores = dot(key_rows[a], jnp.concatenate(wide, 1).astype(BF16))
        return scores, jnp.max(scores, 0, keepdims=True)

    def finish(item, scores, highest):
        a, h = item
        probs = weights_of(scores, highest, depth)
        for k in range(together):
            g = h + k
            values = with_sum_row(both[a][half + g * depth : half + (g + 1) * depth])
            done[a, g] = attended(dot(values, probs[:, k * length : (k + 1) * length]), depth)

    items = [(a, h) for a in range(stripes) for h in range(0, HALF, together)]
    ahead_of(items, score, finish, 2)
    for a in range(stripes):
        attention = jnp.concatenate([done[a, g] for g in range(HALF)], 0).T.astype(BF16)
        here = pl.ds(a * length, length)
        partial[here] = (
            tokens[here].astype(F32) + dot(attention, weight[:half]) + bias[...].reshape(1, 2 * half)
        )


def output_kernel(arrived, partial, weight, output):
    rows, cols, width = output.shape
    half = width // 2
    count = arrived.shape[0]
    across = cols // SPLIT
    down = rows // SPLIT
    square = SPLIT * SPLIT
    each = count // across
    blocks = {}
    for b in range(across):
        lines = jnp.concatenate([arrived[b * each + k].astype(F32) for k in range(each)], 0)
        mixed = dot(lines.T.astype(BF16), weight[half:])
        for a in range(down):
            here = pl.ds((a * across + b) * square, square)
            blocks[a, b] = (partial[here] + mixed[a * square : (a + 1) * square]).reshape(
                SPLIT, SPLIT, width
            )
    for a in range(down):
        output[a * SPLIT : (a + 1) * SPLIT] = jnp.concatenate(
            [blocks[a, b] for b in range(across)], 1
        ).astype(BF16)


def call(kernel, name, out_shape, args, flops, scratch=()):
    moved = sum(x.size * x.dtype.itemsize for x in args)
    return pl.pallas_call(
        kernel,
        out_shape=out_shape,
        in_specs=vmem(len(args)),
        out_specs=jax.tree.map(lambda _: pl.BlockSpec(memory_space=pltpu.VMEM), out_shape),
        scratch_shapes=scratch,
        compiler_params=params(),
        cost_estimate=pl.CostEstimate(flops=flops, bytes_accessed=moved, transcendentals=0),
        name=name,
    )(*args)


def shape(dims, dtype=BF16):
    return jax.ShapeDtypeStruct(dims, dtype)


def gathered(value, axis):
    count = lax.axis_size(axis)
    held = [value]
    for step in range(count - 1, 0, -1):
        pairs = [(k, k ^ step) for k in range(count)]
        held.append(lax.ppermute(value, axis, pairs))
    return held


def exchanged(value, axis):
    count = lax.axis_size(axis)
    lead = 5 * count // 8
    order = [lead] + [k for k in range(count) if k != lead]
    return lax.all_to_all(value, axis, 0, 0, axis_index_groups=[order], tiled=True)


def on_device(
    image,
    conv_weight,
    conv_bias,
    merge_gain,
    merge_shift,
    norm_gain,
    norm_shift,
    qkv_weight,
    proj_weight,
    proj_bias,
):
    in_rows, in_cols, channels = image.shape
    rows, cols = in_rows // 2, in_cols // 2
    width = conv_weight.shape[3]
    half = width // 2
    depth = width // HEADS
    row_count = lax.axis_size("row")
    col_count = lax.axis_size("col")
    down = [(k, k + 1) for k in range(row_count - 1)]
    right = [(k, k + 1) for k in range(col_count - 1)]
    near = 2 * SPLIT
    bottom, side = call(
        edge_kernel,
        "edge",
        (shape((1, in_cols, channels)), shape((in_rows, channels))),
        (image,),
        10**10,
    )
    upper = lax.ppermute(bottom, "row", down)
    pixel_parts = -(-channels // LANES)
    merged = call(
        own_kernel,
        "own_tile",
        shape((rows * cols, width), F32),
        (image, conv_weight),
        10**9,
        [pltpu.VMEM((pixel_parts, in_rows + 1, in_cols + SPLIT, LANES), F32)],
    )
    joined = call(
        join_kernel, "join", shape((in_rows + near, channels)), (side, upper), 10**5
    )
    joined = lax.ppermute(joined, "col", right)
    stripes, across = rows // SPLIT, cols // SPLIT
    per = across * HALF // row_count
    lanes = rows * SPLIT
    tokens, normed, chunks = call(
        merge_kernel,
        "merge",
        (
            shape((rows * cols, width)),
            shape((rows * cols, width)),
            shape((row_count, 3 * per * depth, lanes)),
        ),
        (
            merged,
            upper,
            joined,
            conv_weight,
            qkv_weight,
            conv_bias,
            merge_gain,
            merge_shift,
            norm_gain,
            norm_shift,
        ),
        5 * 10**8,
        [pltpu.VMEM((pixel_parts, 2, max(in_rows, in_cols) + SPLIT, LANES), F32)],
    )
    arrived = exchanged(chunks, "row")
    queries, pairs = call(
        row_qkv_kernel,
        "row_qkv",
        (shape((stripes, half, cols * SPLIT)), shape((stripes, width, cols * SPLIT))),
        (normed, qkv_weight),
        3 * 10**8,
    )
    held = gathered(pairs, "col")
    result = call(
        lambda *refs: col_attention_kernel(depth, *refs),
        "col_attention",
        shape((row_count, per * depth, lanes)),
        (arrived,),
        2 * 10**9,
    )
    back = exchanged(result, "row")
    partial = call(
        lambda *refs: row_attention_kernel(len(held), *refs),
        "row_attention",
        shape((rows * cols, width), F32),
        (queries, *held, tokens, proj_weight, proj_bias),
        2 * 10**9,
    )
    return call(
        output_kernel,
        "output",
        shape((rows, cols, width)),
        (back, partial, proj_weight),
        10**8,
    )


def solution(mesh):
    return jax.shard_map(
        on_device,
        mesh=mesh,
        in_specs=(P("row", "col", None), P(), P(), P(), P(), P(), P(), P(), P(), P()),
        out_specs=P("row", "col", None),
        check_vma=False,
    )
```

```python
import math

import jax
import jax.numpy as jnp
from jax import lax
from jax.experimental import pallas as pl
from jax.experimental.pallas import tpu as pltpu
from jax.sharding import PartitionSpec as P

HEADS = 16
SPLIT = 8
HALF = HEADS // 2
F32 = jnp.float32
BF16 = jnp.bfloat16
LANES = 128


def params():
    return pltpu.CompilerParams(vmem_limit_bytes=48 * 1024 * 1024)


def vmem(count):
    return [pl.BlockSpec(memory_space=pltpu.VMEM)] * count


def dot(left, right):
    return jnp.dot(left, right, preferred_element_type=F32)


def layer_norm(values, gain, shift):
    center = values - jnp.mean(values, -1, keepdims=True)
    spread = jnp.mean(center * center, -1, keepdims=True)
    return center * lax.rsqrt(spread + 1e-05) * gain + shift


def quadrants(rows, cols):
    return [(a, b) for a in range(rows // SPLIT) for b in range(cols // SPLIT)]


def lane_parts(channels):
    return [(k, k * LANES, min(LANES, channels - k * LANES)) for k in range(-(-channels // LANES))]


def every_second(ref, index, first, count, channels):
    return jnp.concatenate(
        [ref[(part, *index, pl.ds(first, count, stride=2))][:, :size] for part, _, size in lane_parts(channels)],
        1,
    )


def edge_kernel(image, bottom, side):
    rows, cols, _ = image.shape
    bottom[...] = image[rows - 1 :]
    side[...] = unless_last(image[:, cols - 2 * SPLIT :].astype(F32)[:, 2 * SPLIT - 1], "col").astype(BF16)


def unless_last(value, axis):
    last = lax.axis_index(axis) == lax.axis_size(axis) - 1
    return jnp.where(last, jnp.zeros_like(value), value)


def join_kernel(bottom, left, joined):
    size = bottom.shape[1]
    extra = joined.shape[0] - size
    joined[:size] = unless_last(bottom[0], "row")
    joined[size:] = unless_last(left[left.shape[0] - extra :], "row")


def own_kernel(image, weight, merged, pixels):
    in_rows, in_cols, channels = image.shape
    rows, cols = in_rows // 2, in_cols // 2
    first = SPLIT
    pixels[:, 0] = jnp.zeros(pixels.shape[:1] + pixels.shape[2:], F32)
    pixels[:, :, :first] = jnp.zeros(pixels.shape[:2] + (first, LANES), F32)
    for part, start, size in lane_parts(channels):
        pixels[part, pl.ds(1, in_rows), pl.ds(first, in_cols), pl.ds(0, size)] = image[
            :, :, pl.ds(start, size)
        ].astype(F32)
    total = jnp.zeros((rows * cols, merged.shape[1]), F32)
    for tap in range(3):
        lines = [
            every_second(pixels, (i,), first - 1 + tap, cols, channels).astype(BF16)
            for i in range(in_rows + 1)
        ]
        for tap_row in range(3):
            window = jnp.concatenate(lines[tap_row : tap_row + 2 * rows - 1 : 2], 0)
            total = total + dot(window, weight[tap_row, tap])
    merged[...] = total


def merge_kernel(
    merged, left, joined, weight, qkv, bias, gain, shift, gain2, shift2, tokens, normed, chunks, edges
):
    in_rows, channels = left.shape
    in_cols = 4 * merged.shape[0] // in_rows
    rows, cols = in_rows // 2, in_cols // 2
    width = weight.shape[3]
    depth = width // HEADS
    first = SPLIT
    row = lambda ref: ref[...].reshape(1, width)
    for part, start, size in lane_parts(channels):
        lanes, here = pl.ds(0, size), pl.ds(start, size)
        upper = joined[:, here].astype(F32)
        edges[part, 0, pl.ds(first, in_cols), lanes] = upper[:in_cols]
        edges[part, 0, pl.ds(first - 1, 1), lanes] = upper[upper.shape[0] - 1 :]
        edges[part, 1, pl.ds(first, in_rows), lanes] = left[:, here].astype(F32)
        edges[part, 1, pl.ds(first - 1, 1), lanes] = jnp.zeros((1, size), F32)
    above = [every_second(edges, (0,), first - 1 + tap, cols, channels).astype(BF16) for tap in range(3)]
    aside = [every_second(edges, (1,), first - 1 + tap, rows, channels).astype(BF16) for tap in range(3)]
    corner = dot(jnp.concatenate([above[0], aside[0]], 0), weight[0, 0])
    top = corner[:cols] + dot(above[1], weight[0, 1]) + dot(above[2], weight[0, 2])
    near = corner[cols:] + dot(aside[1], weight[1, 0]) + dot(aside[2], weight[2, 0])
    grid = merged[...].reshape(rows, cols, width)
    grid = jnp.concatenate([grid[:1] + top.reshape(1, cols, width), grid[1:]], 0)
    begin = lax.broadcasted_iota(jnp.int32, (rows, SPLIT, width), 1) == 0
    grid = jnp.concatenate(
        [grid[:, :SPLIT] + jnp.where(begin, near.reshape(rows, 1, width), 0.0), grid[:, SPLIT:]], 1
    )
    grid = jnp.concatenate(
        [
            grid[a * SPLIT : (a + 1) * SPLIT, b * SPLIT : (b + 1) * SPLIT].reshape(SPLIT * SPLIT, width)
            for a, b in quadrants(rows, cols)
        ],
        0,
    )
    held = layer_norm(grid + row(bias), row(gain), row(shift)).astype(BF16)
    tokens[...] = held
    again = layer_norm(held.astype(F32), row(gain2), row(shift2)).astype(BF16)
    normed[...] = again
    across = cols // SPLIT
    count = chunks.shape[0]
    per = across * HALF // count
    square = SPLIT * SPLIT
    for b in range(across):
        mine = [
            again[(a * across + b) * square : (a * across + b + 1) * square] for a in range(rows // SPLIT)
        ]
        mine = jnp.concatenate(mine, 0)
        lines = []
        for kind in range(3):
            begin = kind * width + width // 2
            base = begin // LANES * LANES
            wide = dot(mine, qkv[:, base : (kind + 1) * width])
            lines.append(wide.T[begin - base :])
        for item in range(b * HALF, (b + 1) * HALF, per):
            low = (item - b * HALF) * depth
            chunks[item // per] = jnp.concatenate(
                [kind[low : low + per * depth] for kind in lines], 0
            ).astype(BF16)


def row_qkv_kernel(normed, qkv, queries, pairs):
    width = normed.shape[1]
    half = width // 2
    step = normed.shape[0] // queries.shape[0]
    for a in range(queries.shape[0]):
        mine = normed[a * step : (a + 1) * step]
        for kind in range(3):
            begin = kind * width
            end = begin + -(-half // LANES) * LANES
            lines = dot(mine, qkv[:, begin:end]).T[:half].astype(BF16)
            if kind == 0:
                queries[a] = lines
            else:
                pairs[a, (kind - 1) * half : kind * half] = lines


def padded_rows(values, start, total):
    size, lanes = values.shape
    pieces = []
    if start:
        pieces.append(jnp.zeros((start, lanes), F32))
    pieces.append(values)
    if total - start - size:
        pieces.append(jnp.zeros((total - start - size, lanes), F32))
    return jnp.concatenate(pieces, 0)


def with_sum_row(values):
    lanes = values.shape[1]
    return jnp.concatenate(
        [values, jnp.ones((1, lanes), F32), jnp.zeros((7, lanes), F32)], 0
    ).astype(BF16)


def weights_of(scores, highest, depth):
    return jnp.exp2((scores - highest) * (math.log2(math.e) / math.sqrt(depth))).astype(BF16)


def ahead_of(items, score, finish, ahead):
    waiting = [score(item) for item in items[:ahead]]
    for k, item in enumerate(items):
        if k + ahead < len(items):
            waiting.append(score(items[k + ahead]))
        finish(item, *waiting.pop(0))


def attended(mixed, depth):
    return mixed[:depth] / mixed[depth : depth + 1]


def col_attention_kernel(depth, arrived, result):
    count, lines, length = arrived.shape
    per = lines // (3 * depth)
    total = per * depth
    lanes = jnp.concatenate([arrived[s].astype(F32) for s in range(count)], 1)
    key_rows = lanes[total : 2 * total].T.astype(BF16)
    values = [
        with_sum_row(lanes[2 * total + h * depth : 2 * total + (h + 1) * depth]) for h in range(per)
    ]
    block = 4 * length
    done = {}

    def score(item):
        begin, h = item
        queries = padded_rows(lanes[h * depth : (h + 1) * depth, begin : begin + block], h * depth, total)
        scores = dot(key_rows, queries.astype(BF16))
        return scores, jnp.max(scores, 0, keepdims=True)

    def finish(item, scores, highest):
        done[item] = attended(dot(values[item[1]], weights_of(scores, highest, depth)), depth)

    starts = range(0, count * length, block)
    ahead_of([(begin, h) for begin in starts for h in range(per)], score, finish, 1)
    for begin in starts:
        heads = jnp.concatenate([done[begin, h] for h in range(per)], 0).astype(BF16)
        for k in range(block // length):
            result[begin // length + k] = heads[:, k * length : (k + 1) * length]


def row_attention_kernel(count, queries, *refs):
    pairs = refs[:count]
    tokens, weight, bias, partial = refs[count:]
    stripes, half, length = queries.shape
    depth = half // HALF
    together = 2
    both, key_rows, lines, done = [], [], [], {}
    for a in range(stripes):
        both.append(jnp.concatenate([ref[a].astype(F32) for ref in pairs], 1))
        key_rows.append(both[a][:half].T.astype(BF16))
        lines.append(queries[a].astype(F32))

    def score(item):
        a, h = item
        wide = [
            padded_rows(lines[a][g * depth : (g + 1) * depth], g * depth, half)
            for g in range(h, h + together)
        ]
        scores = dot(key_rows[a], jnp.concatenate(wide, 1).astype(BF16))
        return scores, jnp.max(scores, 0, keepdims=True)

    def finish(item, scores, highest):
        a, h = item
        probs = weights_of(scores, highest, depth)
        for k in range(together):
            g = h + k
            values = with_sum_row(both[a][half + g * depth : half + (g + 1) * depth])
            done[a, g] = attended(dot(values, probs[:, k * length : (k + 1) * length]), depth)

    items = [(a, h) for a in range(stripes) for h in range(0, HALF, together)]
    ahead_of(items, score, finish, 2)
    for a in range(stripes):
        attention = jnp.concatenate([done[a, g] for g in range(HALF)], 0).T.astype(BF16)
        here = pl.ds(a * length, length)
        partial[here] = (
            tokens[here].astype(F32) + dot(attention, weight[:half]) + bias[...].reshape(1, 2 * half)
        )


def output_kernel(arrived, partial, weight, output):
    rows, cols, width = output.shape
    half = width // 2
    count = arrived.shape[0]
    across = cols // SPLIT
    down = rows // SPLIT
    square = SPLIT * SPLIT
    each = count // across
    blocks = {}
    for b in range(across):
        lines = jnp.concatenate([arrived[b * each + k].astype(F32) for k in range(each)], 0)
        mixed = dot(lines.T.astype(BF16), weight[half:])
        for a in range(down):
            here = pl.ds((a * across + b) * square, square)
            blocks[a, b] = (partial[here] + mixed[a * square : (a + 1) * square]).reshape(
                SPLIT, SPLIT, width
            )
    for a in range(down):
        output[a * SPLIT : (a + 1) * SPLIT] = jnp.concatenate(
            [blocks[a, b] for b in range(across)], 1
        ).astype(BF16)


def call(kernel, name, out_shape, args, flops, scratch=()):
    moved = sum(x.size * x.dtype.itemsize for x in args)
    return pl.pallas_call(
        kernel,
        out_shape=out_shape,
        in_specs=vmem(len(args)),
        out_specs=jax.tree.map(lambda _: pl.BlockSpec(memory_space=pltpu.VMEM), out_shape),
        scratch_shapes=scratch,
        compiler_params=params(),
        cost_estimate=pl.CostEstimate(flops=flops, bytes_accessed=moved, transcendentals=0),
        name=name,
    )(*args)


def shape(dims, dtype=BF16):
    return jax.ShapeDtypeStruct(dims, dtype)


def gathered(value, axis):
    count = lax.axis_size(axis)
    held = [value]
    for step in range(count - 1, 0, -1):
        pairs = [(k, k ^ step) for k in range(count)]
        held.append(lax.ppermute(value, axis, pairs))
    return held


def exchanged(value, axis):
    count = lax.axis_size(axis)
    lead = 5 * count // 8
    order = [lead] + [k for k in range(count) if k != lead]
    return lax.all_to_all(value, axis, 0, 0, axis_index_groups=[order], tiled=True)


def on_device(
    image,
    conv_weight,
    conv_bias,
    merge_gain,
    merge_shift,
    norm_gain,
    norm_shift,
    qkv_weight,
    proj_weight,
    proj_bias,
):
    in_rows, in_cols, channels = image.shape
    rows, cols = in_rows // 2, in_cols // 2
    width = conv_weight.shape[3]
    half = width // 2
    depth = width // HEADS
    row_count = lax.axis_size("row")
    col_count = lax.axis_size("col")
    down = [(k, (k + 1) % row_count) for k in range(row_count)]
    right = [(k, (k + 1) % col_count) for k in range(col_count)]
    near = 2 * SPLIT
    bottom, side = call(
        edge_kernel,
        "edge",
        (shape((1, in_cols, channels)), shape((in_rows, channels))),
        (image,),
        10**10,
    )
    left = lax.ppermute(side, "col", right)
    pixel_parts = -(-channels // LANES)
    merged = call(
        own_kernel,
        "own_tile",
        shape((rows * cols, width), F32),
        (image, conv_weight),
        10**9,
        [pltpu.VMEM((pixel_parts, in_rows + 1, in_cols + SPLIT, LANES), F32)],
    )
    joined = call(
        join_kernel, "join", shape((in_cols + near, channels)), (bottom, left), 10**5
    )
    joined = lax.ppermute(joined, "row", down)
    stripes, across = rows // SPLIT, cols // SPLIT
    per = across * HALF // row_count
    lanes = rows * SPLIT
    tokens, normed, chunks = call(
        merge_kernel,
        "merge",
        (
            shape((rows * cols, width)),
            shape((rows * cols, width)),
            shape((row_count, 3 * per * depth, lanes)),
        ),
        (
            merged,
            left,
            joined,
            conv_weight,
            qkv_weight,
            conv_bias,
            merge_gain,
            merge_shift,
            norm_gain,
            norm_shift,
        ),
        5 * 10**8,
        [pltpu.VMEM((pixel_parts, 2, max(in_rows, in_cols) + SPLIT, LANES), F32)],
    )
    arrived = exchanged(chunks, "row")
    queries, pairs = call(
        row_qkv_kernel,
        "row_qkv",
        (shape((stripes, half, cols * SPLIT)), shape((stripes, width, cols * SPLIT))),
        (normed, qkv_weight),
        3 * 10**8,
    )
    held = gathered(pairs, "col")
    result = call(
        lambda *refs: col_attention_kernel(depth, *refs),
        "col_attention",
        shape((row_count, per * depth, lanes)),
        (arrived,),
        2 * 10**9,
    )
    back = exchanged(result, "row")
    partial = call(
        lambda *refs: row_attention_kernel(len(held), *refs),
        "row_attention",
        shape((rows * cols, width), F32),
        (queries, *held, tokens, proj_weight, proj_bias),
        2 * 10**9,
    )
    return call(
        output_kernel,
        "output",
        shape((rows, cols, width)),
        (back, partial, proj_weight),
        10**8,
    )


def solution(mesh):
    return jax.shard_map(
        on_device,
        mesh=mesh,
        in_specs=(P("row", "col", None), P(), P(), P(), P(), P(), P(), P(), P(), P()),
        out_specs=P("row", "col", None),
        check_vma=False,
    )
```

```python
import math

import jax
import jax.numpy as jnp
from jax import lax
from jax.experimental import pallas as pl
from jax.experimental.pallas import tpu as pltpu
from jax.sharding import PartitionSpec as P

HEADS = 16
SPLIT = 8
HALF = HEADS // 2
F32 = jnp.float32
BF16 = jnp.bfloat16
LANES = 128


def params():
    return pltpu.CompilerParams(vmem_limit_bytes=48 * 1024 * 1024)


def vmem(count):
    return [pl.BlockSpec(memory_space=pltpu.VMEM)] * count


def dot(left, right):
    return jnp.dot(left, right, preferred_element_type=F32)


def layer_norm(values, gain, shift):
    center = values - jnp.mean(values, -1, keepdims=True)
    spread = jnp.mean(center * center, -1, keepdims=True)
    return center * lax.rsqrt(spread + 1e-05) * gain + shift


def quadrants(rows, cols):
    return [(a, b) for a in range(rows // SPLIT) for b in range(cols // SPLIT)]


def lane_parts(channels):
    return [(k, k * LANES, min(LANES, channels - k * LANES)) for k in range(-(-channels // LANES))]


def every_second(ref, index, first, count, channels):
    return jnp.concatenate(
        [ref[(part, *index, pl.ds(first, count, stride=2))][:, :size] for part, _, size in lane_parts(channels)],
        1,
    )


def unless_last(value, axis):
    last = lax.axis_index(axis) == lax.axis_size(axis) - 1
    return jnp.where(last, jnp.zeros_like(value), value)


def edge_kernel(image, bottom, side):
    rows, cols, _ = image.shape
    near = 2 * SPLIT
    bottom[...] = unless_last(image[rows - 1], "row")
    side[...] = unless_last(image[:, cols - near :].astype(F32)[:, near - 1], "col").astype(BF16)


def corner_kernel(bottom, corner):
    corner[...] = unless_last(bottom[bottom.shape[0] - corner.shape[0] :], "col")


def own_kernel(image, weight, merged, pixels):
    in_rows, in_cols, channels = image.shape
    rows, cols = in_rows // 2, in_cols // 2
    first = SPLIT
    pixels[:, 0] = jnp.zeros(pixels.shape[:1] + pixels.shape[2:], F32)
    pixels[:, :, :first] = jnp.zeros(pixels.shape[:2] + (first, LANES), F32)
    for part, start, size in lane_parts(channels):
        pixels[part, pl.ds(1, in_rows), pl.ds(first, in_cols), pl.ds(0, size)] = image[
            :, :, pl.ds(start, size)
        ].astype(F32)
    total = jnp.zeros((rows * cols, merged.shape[1]), F32)
    for tap in range(3):
        lines = [
            every_second(pixels, (i,), first - 1 + tap, cols, channels).astype(BF16)
            for i in range(in_rows + 1)
        ]
        for tap_row in range(3):
            window = jnp.concatenate(lines[tap_row : tap_row + 2 * rows - 1 : 2], 0)
            total = total + dot(window, weight[tap_row, tap])
    merged[...] = total


def merge_kernel(
    merged, upper, left, corner, weight, qkv, bias, gain, shift, gain2, shift2, tokens, normed, chunks, edges, held_chunks, sems
):
    in_rows, channels = left.shape
    in_cols = 4 * merged.shape[0] // in_rows
    rows, cols = in_rows // 2, in_cols // 2
    width = weight.shape[3]
    depth = width // HEADS
    first = SPLIT
    row = lambda ref: ref[...].reshape(1, width)
    for part, start, size in lane_parts(channels):
        lanes, here = pl.ds(0, size), pl.ds(start, size)
        edges[part, 0, pl.ds(first, in_cols), lanes] = upper[:, here].astype(F32)
        edges[part, 0, pl.ds(first - 1, 1), lanes] = corner[:, here].astype(F32)[corner.shape[0] - 1 :]
        edges[part, 1, pl.ds(first, in_rows), lanes] = left[:, here].astype(F32)
        edges[part, 1, pl.ds(first - 1, 1), lanes] = jnp.zeros((1, size), F32)
    above = [every_second(edges, (0,), first - 1 + tap, cols, channels).astype(BF16) for tap in range(3)]
    aside = [every_second(edges, (1,), first - 1 + tap, rows, channels).astype(BF16) for tap in range(3)]
    corner = dot(jnp.concatenate([above[0], aside[0]], 0), weight[0, 0])
    top = corner[:cols] + dot(above[1], weight[0, 1]) + dot(above[2], weight[0, 2])
    near = corner[cols:] + dot(aside[1], weight[1, 0]) + dot(aside[2], weight[2, 0])
    grid = merged[...].reshape(rows, cols, width)
    grid = jnp.concatenate([grid[:1] + top.reshape(1, cols, width), grid[1:]], 0)
    begin = lax.broadcasted_iota(jnp.int32, (rows, SPLIT, width), 1) == 0
    grid = jnp.concatenate(
        [grid[:, :SPLIT] + jnp.where(begin, near.reshape(rows, 1, width), 0.0), grid[:, SPLIT:]], 1
    )
    grid = jnp.concatenate(
        [
            grid[a * SPLIT : (a + 1) * SPLIT, b * SPLIT : (b + 1) * SPLIT].reshape(SPLIT * SPLIT, width)
            for a, b in quadrants(rows, cols)
        ],
        0,
    )
    held = layer_norm(grid + row(bias), row(gain), row(shift)).astype(BF16)
    tokens[...] = held
    again = layer_norm(held.astype(F32), row(gain2), row(shift2)).astype(BF16)
    normed[...] = again
    across = cols // SPLIT
    count = chunks.shape[0]
    per = across * HALF // count
    square = SPLIT * SPLIT
    copies = [pltpu.make_async_copy(held_chunks.at[k], chunks.at[k], sems.at[k]) for k in range(count)]
    for b in range(across):
        mine = [
            again[(a * across + b) * square : (a * across + b + 1) * square] for a in range(rows // SPLIT)
        ]
        mine = jnp.concatenate(mine, 0)
        lines = []
        for kind in range(3):
            begin = kind * width + width // 2
            base = begin // LANES * LANES
            wide = dot(mine, qkv[:, base : (kind + 1) * width])
            lines.append(wide.T[begin - base :])
        for item in range(b * HALF, (b + 1) * HALF, per):
            low = (item - b * HALF) * depth
            held_chunks[item // per] = jnp.concatenate(
                [kind[low : low + per * depth] for kind in lines], 0
            ).astype(BF16)
            copies[item // per].start()
    for copy in copies:
        copy.wait()


def row_qkv_kernel(normed, qkv, queries, pairs):
    width = normed.shape[1]
    half = width // 2
    step = normed.shape[0] // queries.shape[0]
    for a in range(queries.shape[0]):
        mine = normed[a * step : (a + 1) * step]
        for kind in range(3):
            begin = kind * width
            end = begin + -(-half // LANES) * LANES
            lines = dot(mine, qkv[:, begin:end]).T[:half].astype(BF16)
            if kind == 0:
                queries[a] = lines
            else:
                pairs[a, (kind - 1) * half : kind * half] = lines


def padded_rows(values, start, total):
    size, lanes = values.shape
    pieces = []
    if start:
        pieces.append(jnp.zeros((start, lanes), F32))
    pieces.append(values)
    if total - start - size:
        pieces.append(jnp.zeros((total - start - size, lanes), F32))
    return jnp.concatenate(pieces, 0)


def with_sum_row(values):
    lanes = values.shape[1]
    return jnp.concatenate(
        [values, jnp.ones((1, lanes), F32), jnp.zeros((7, lanes), F32)], 0
    ).astype(BF16)


def weights_of(scores, highest, depth):
    return jnp.exp2((scores - highest) * (math.log2(math.e) / math.sqrt(depth))).astype(BF16)


def ahead_of(items, score, finish, ahead):
    waiting = [score(item) for item in items[:ahead]]
    for k, item in enumerate(items):
        if k + ahead < len(items):
            waiting.append(score(items[k + ahead]))
        finish(item, *waiting.pop(0))


def attended(mixed, depth):
    return mixed[:depth] / mixed[depth : depth + 1]


def col_attention_kernel(depth, arrived, result, done, sems):
    count, lines, length = arrived.shape
    per = lines // (3 * depth)
    total = per * depth
    lanes = jnp.concatenate([arrived[s].astype(F32) for s in range(count)], 1)
    key_rows = lanes[total : 2 * total].astype(BF16).T
    values = [
        with_sum_row(lanes[2 * total + h * depth : 2 * total + (h + 1) * depth]) for h in range(per)
    ]
    block = 2 * length
    copies = [pltpu.make_async_copy(done.at[k], result.at[k], sems.at[k]) for k in range(count)]
    heads = []

    def score(item):
        begin, h = item
        queries = padded_rows(lanes[h * depth : (h + 1) * depth, begin : begin + block], h * depth, total)
        scores = dot(key_rows, queries.astype(BF16))
        return scores, jnp.max(scores, 0, keepdims=True)

    def finish(item, scores, highest):
        begin, h = item
        heads.append(attended(dot(values[h], weights_of(scores, highest, depth)), depth))
        if h == per - 1:
            both = jnp.concatenate(heads, 0).astype(BF16)
            heads.clear()
            for k in range(begin // length, (begin + block) // length):
                done[k] = both[:, k * length - begin : (k + 1) * length - begin]
                copies[k].start()

    ahead_of([(begin, h) for begin in range(0, count * length, block) for h in range(per)], score, finish, 3)
    for copy in copies:
        copy.wait()


def row_attention_kernel(count, queries, *refs):
    pairs = refs[:count]
    tokens, weight, bias, partial = refs[count:]
    stripes, half, length = queries.shape
    depth = half // HALF
    together = 2
    both, key_rows, lines, done = [], [], [], {}
    for a in range(stripes):
        both.append(jnp.concatenate([ref[a].astype(F32) for ref in pairs], 1))
        key_rows.append(both[a][:half].T.astype(BF16))
        lines.append(queries[a].astype(F32))

    def score(item):
        a, h = item
        wide = [
            padded_rows(lines[a][g * depth : (g + 1) * depth], g * depth, half)
            for g in range(h, h + together)
        ]
        scores = dot(key_rows[a], jnp.concatenate(wide, 1).astype(BF16))
        return scores, jnp.max(scores, 0, keepdims=True)

    def finish(item, scores, highest):
        a, h = item
        probs = weights_of(scores, highest, depth)
        for k in range(together):
            g = h + k
            values = with_sum_row(both[a][half + g * depth : half + (g + 1) * depth])
            done[a, g] = attended(dot(values, probs[:, k * length : (k + 1) * length]), depth)

    items = [(a, h) for a in range(stripes) for h in range(0, HALF, together)]
    ahead_of(items, score, finish, 2)
    for a in range(stripes):
        attention = jnp.concatenate([done[a, g] for g in range(HALF)], 0).T.astype(BF16)
        here = pl.ds(a * length, length)
        partial[here] = (
            tokens[here].astype(F32) + dot(attention, weight[:half]) + bias[...].reshape(1, 2 * half)
        )


def output_kernel(arrived, partial, weight, output):
    rows, cols, width = output.shape
    half = width // 2
    count = arrived.shape[0]
    across = cols // SPLIT
    down = rows // SPLIT
    square = SPLIT * SPLIT
    each = count // across
    blocks = {}
    for b in range(across):
        lines = jnp.concatenate([arrived[b * each + k].astype(F32) for k in range(each)], 0)
        mixed = dot(lines.T.astype(BF16), weight[half:])
        for a in range(down):
            here = pl.ds((a * across + b) * square, square)
            blocks[a, b] = (partial[here] + mixed[a * square : (a + 1) * square]).reshape(
                SPLIT, SPLIT, width
            )
    for a in range(down):
        output[a * SPLIT : (a + 1) * SPLIT] = jnp.concatenate(
            [blocks[a, b] for b in range(across)], 1
        ).astype(BF16)


def call(kernel, name, out_shape, args, flops, scratch=(), loose=()):
    several = isinstance(out_shape, tuple)
    spaces = [pl.ANY if k in loose else pltpu.VMEM for k in range(len(out_shape) if several else 1)]
    specs = tuple(pl.BlockSpec(memory_space=space) for space in spaces)
    moved = sum(x.size * x.dtype.itemsize for x in args)
    return pl.pallas_call(
        kernel,
        out_shape=out_shape,
        in_specs=vmem(len(args)),
        out_specs=specs if several else specs[0],
        scratch_shapes=scratch,
        compiler_params=params(),
        cost_estimate=pl.CostEstimate(flops=flops, bytes_accessed=moved, transcendentals=0),
        name=name,
    )(*args)


def shape(dims, dtype=BF16):
    return jax.ShapeDtypeStruct(dims, dtype)


def gathered(value, axis):
    count = lax.axis_size(axis)
    held = [value]
    for step in range(count - 1, 0, -1):
        pairs = [(k, k ^ step) for k in range(count)]
        held.append(lax.ppermute(value, axis, pairs))
    return held


def exchanged(value, axis):
    count = lax.axis_size(axis)
    lead = 5 * count // 8
    order = [lead] + [k for k in range(count) if k != lead]
    return lax.all_to_all(value, axis, 0, 0, axis_index_groups=[order], tiled=True)


def on_device(
    image,
    conv_weight,
    conv_bias,
    merge_gain,
    merge_shift,
    norm_gain,
    norm_shift,
    qkv_weight,
    proj_weight,
    proj_bias,
):
    in_rows, in_cols, channels = image.shape
    rows, cols = in_rows // 2, in_cols // 2
    width = conv_weight.shape[3]
    half = width // 2
    depth = width // HEADS
    row_count = lax.axis_size("row")
    col_count = lax.axis_size("col")
    down = [(k, (k + 1) % row_count) for k in range(row_count)]
    right = [(k, (k + 1) % col_count) for k in range(col_count)]
    diagonal = []
    for r in range(row_count):
        for c in range(col_count):
            target = (r, 0) if c == col_count - 1 else ((r + 1) % row_count, c + 1)
            diagonal.append((r * col_count + c, target[0] * col_count + target[1]))
    near = 2 * SPLIT
    bottom, side = call(
        edge_kernel,
        "edge",
        (shape((in_cols, channels)), shape((in_rows, channels))),
        (image,),
        10**5,
    )
    corner = call(corner_kernel, "corner", shape((near, channels)), (bottom,), 10**10)
    upper = lax.ppermute(bottom, "row", down)
    left = lax.ppermute(side, "col", right)
    corner = lax.ppermute(corner, ("row", "col"), diagonal)
    pixel_parts = -(-channels // LANES)
    merged = call(
        own_kernel,
        "own_tile",
        shape((rows * cols, width), F32),
        (image, conv_weight),
        10**9,
        [pltpu.VMEM((pixel_parts, in_rows + 1, in_cols + SPLIT, LANES), F32)],
    )
    stripes, across = rows // SPLIT, cols // SPLIT
    per = across * HALF // row_count
    lanes = rows * SPLIT
    tokens, normed, chunks = call(
        merge_kernel,
        "merge",
        (
            shape((rows * cols, width)),
            shape((rows * cols, width)),
            shape((row_count, 3 * per * depth, lanes)),
        ),
        (
            merged,
            upper,
            left,
            corner,
            conv_weight,
            qkv_weight,
            conv_bias,
            merge_gain,
            merge_shift,
            norm_gain,
            norm_shift,
        ),
        5 * 10**8,
        [
            pltpu.VMEM((pixel_parts, 2, max(in_rows, in_cols) + SPLIT, LANES), F32),
            pltpu.VMEM((row_count, 3 * per * depth, lanes), BF16),
            pltpu.SemaphoreType.DMA((row_count,)),
        ],
        (2,),
    )
    arrived = exchanged(chunks, "row")
    queries, pairs = call(
        row_qkv_kernel,
        "row_qkv",
        (shape((stripes, half, cols * SPLIT)), shape((stripes, width, cols * SPLIT))),
        (normed, qkv_weight),
        3 * 10**8,
    )
    held = gathered(pairs, "col")
    result = call(
        lambda *refs: col_attention_kernel(depth, *refs),
        "col_attention",
        shape((row_count, per * depth, lanes)),
        (arrived,),
        2 * 10**9,
        [pltpu.VMEM((row_count, per * depth, lanes), BF16), pltpu.SemaphoreType.DMA((row_count,))],
        (0,),
    )
    back = exchanged(result, "row")
    partial = call(
        lambda *refs: row_attention_kernel(len(held), *refs),
        "row_attention",
        shape((rows * cols, width), F32),
        (queries, *held, tokens, proj_weight, proj_bias),
        2 * 10**9,
    )
    return call(
        output_kernel,
        "output",
        shape((rows, cols, width)),
        (back, partial, proj_weight),
        10**8,
    )


def solution(mesh):
    return jax.shard_map(
        on_device,
        mesh=mesh,
        in_specs=(P("row", "col", None), P(), P(), P(), P(), P(), P(), P(), P(), P()),
        out_specs=P("row", "col", None),
        check_vma=False,
    )
```

```python
import math

import jax
import jax.numpy as jnp
from jax import lax
from jax.experimental import pallas as pl
from jax.experimental.pallas import tpu as pltpu
from jax.sharding import PartitionSpec as P

HEADS = 16
SPLIT = 8
HALF = HEADS // 2
F32 = jnp.float32
BF16 = jnp.bfloat16
LANES = 128


def params():
    return pltpu.CompilerParams(vmem_limit_bytes=48 * 1024 * 1024)


def vmem(count):
    return [pl.BlockSpec(memory_space=pltpu.VMEM)] * count


def dot(left, right):
    return jnp.dot(left, right, preferred_element_type=F32)


def layer_norm(values, gain, shift):
    center = values - jnp.mean(values, -1, keepdims=True)
    spread = jnp.mean(center * center, -1, keepdims=True)
    return center * lax.rsqrt(spread + 1e-05) * gain + shift


def quadrants(rows, cols):
    return [(a, b) for a in range(rows // SPLIT) for b in range(cols // SPLIT)]


def lane_parts(channels):
    return [(k, k * LANES, min(LANES, channels - k * LANES)) for k in range(-(-channels // LANES))]


def every_second(ref, index, first, count, channels):
    return jnp.concatenate(
        [ref[(part, *index, pl.ds(first, count, stride=2))][:, :size] for part, _, size in lane_parts(channels)],
        1,
    )


def edge_kernel(image, side):
    near = 2 * SPLIT
    side[...] = image[:, image.shape[1] - near :].astype(F32)[:, near - 1].astype(BF16)


def corner_kernel(bottom, corner):
    corner[...] = bottom[bottom.shape[0] - corner.shape[0] :]


def own_kernel(image, weight, merged, pixels):
    in_rows, in_cols, channels = image.shape
    rows, cols = in_rows // 2, in_cols // 2
    first = SPLIT
    pixels[:, 0] = jnp.zeros(pixels.shape[:1] + pixels.shape[2:], F32)
    pixels[:, :, :first] = jnp.zeros(pixels.shape[:2] + (first, LANES), F32)
    for part, start, size in lane_parts(channels):
        pixels[part, pl.ds(1, in_rows), pl.ds(first, in_cols), pl.ds(0, size)] = image[
            :, :, pl.ds(start, size)
        ].astype(F32)
    total = jnp.zeros((rows * cols, merged.shape[1]), F32)
    for tap in range(3):
        lines = [
            every_second(pixels, (i,), first - 1 + tap, cols, channels).astype(BF16)
            for i in range(in_rows + 1)
        ]
        for tap_row in range(3):
            window = jnp.concatenate(lines[tap_row : tap_row + 2 * rows - 1 : 2], 0)
            total = total + dot(window, weight[tap_row, tap])
    merged[...] = total


def kept(value, axis):
    return jnp.where(lax.axis_index(axis) == 0, jnp.zeros(value.shape, F32), value.astype(F32))


def merge_kernel(
    merged, upper, left, corner, weight, qkv, bias, gain, shift, gain2, shift2, tokens, normed, chunks, edges, held_chunks, sems
):
    in_rows, channels = left.shape
    in_cols = 4 * merged.shape[0] // in_rows
    rows, cols = in_rows // 2, in_cols // 2
    width = weight.shape[3]
    depth = width // HEADS
    first = SPLIT
    row = lambda ref: ref[...].reshape(1, width)
    for part, start, size in lane_parts(channels):
        lanes, here = pl.ds(0, size), pl.ds(start, size)
        edges[part, 0, pl.ds(first, in_cols), lanes] = kept(upper[:, here], "row")
        edges[part, 0, pl.ds(first - 1, 1), lanes] = kept(kept(corner[:, here], "row")[corner.shape[0] - 1 :], "col")
        edges[part, 1, pl.ds(first, in_rows), lanes] = kept(left[:, here], "col")
        edges[part, 1, pl.ds(first - 1, 1), lanes] = jnp.zeros((1, size), F32)
    above = [every_second(edges, (0,), first - 1 + tap, cols, channels).astype(BF16) for tap in range(3)]
    aside = [every_second(edges, (1,), first - 1 + tap, rows, channels).astype(BF16) for tap in range(3)]
    corner = dot(jnp.concatenate([above[0], aside[0]], 0), weight[0, 0])
    top = corner[:cols] + dot(above[1], weight[0, 1]) + dot(above[2], weight[0, 2])
    near = corner[cols:] + dot(aside[1], weight[1, 0]) + dot(aside[2], weight[2, 0])
    grid = merged[...].reshape(rows, cols, width)
    grid = jnp.concatenate([grid[:1] + top.reshape(1, cols, width), grid[1:]], 0)
    begin = lax.broadcasted_iota(jnp.int32, (rows, SPLIT, width), 1) == 0
    grid = jnp.concatenate(
        [grid[:, :SPLIT] + jnp.where(begin, near.reshape(rows, 1, width), 0.0), grid[:, SPLIT:]], 1
    )
    grid = jnp.concatenate(
        [
            grid[a * SPLIT : (a + 1) * SPLIT, b * SPLIT : (b + 1) * SPLIT].reshape(SPLIT * SPLIT, width)
            for a, b in quadrants(rows, cols)
        ],
        0,
    )
    held = layer_norm(grid + row(bias), row(gain), row(shift)).astype(BF16)
    tokens[...] = held
    again = layer_norm(held.astype(F32), row(gain2), row(shift2)).astype(BF16)
    normed[...] = again
    across = cols // SPLIT
    count = chunks.shape[0]
    per = across * HALF // count
    square = SPLIT * SPLIT
    copies = [pltpu.make_async_copy(held_chunks.at[k], chunks.at[k], sems.at[k]) for k in range(count)]
    for b in range(across):
        mine = [
            again[(a * across + b) * square : (a * across + b + 1) * square] for a in range(rows // SPLIT)
        ]
        mine = jnp.concatenate(mine, 0)
        lines = []
        for kind in range(3):
            begin = kind * width + width // 2
            base = begin // LANES * LANES
            wide = dot(mine, qkv[:, base : (kind + 1) * width])
            lines.append(wide.T[begin - base :])
        for item in range(b * HALF, (b + 1) * HALF, per):
            low = (item - b * HALF) * depth
            held_chunks[item // per] = jnp.concatenate(
                [kind[low : low + per * depth] for kind in lines], 0
            ).astype(BF16)
            copies[item // per].start()
    for copy in copies:
        copy.wait()


def row_qkv_kernel(normed, qkv, queries, pairs):
    width = normed.shape[1]
    half = width // 2
    step = normed.shape[0] // queries.shape[0]
    for a in range(queries.shape[0]):
        mine = normed[a * step : (a + 1) * step]
        for kind in range(3):
            begin = kind * width
            end = begin + -(-half // LANES) * LANES
            lines = dot(mine, qkv[:, begin:end]).T[:half].astype(BF16)
            if kind == 0:
                queries[a] = lines
            else:
                pairs[a, (kind - 1) * half : kind * half] = lines


def padded_rows(values, start, total):
    size, lanes = values.shape
    pieces = []
    if start:
        pieces.append(jnp.zeros((start, lanes), F32))
    pieces.append(values)
    if total - start - size:
        pieces.append(jnp.zeros((total - start - size, lanes), F32))
    return jnp.concatenate(pieces, 0)


def with_sum_row(values):
    lanes = values.shape[1]
    return jnp.concatenate(
        [values, jnp.ones((1, lanes), F32), jnp.zeros((7, lanes), F32)], 0
    ).astype(BF16)


def weights_of(scores, highest, depth):
    return jnp.exp2((scores - highest) * (math.log2(math.e) / math.sqrt(depth))).astype(BF16)


def ahead_of(items, score, finish, ahead):
    waiting = [score(item) for item in items[:ahead]]
    for k, item in enumerate(items):
        if k + ahead < len(items):
            waiting.append(score(items[k + ahead]))
        finish(item, *waiting.pop(0))


def attended(mixed, depth):
    return mixed[:depth] / mixed[depth : depth + 1]


def col_attention_kernel(depth, arrived, result, done, sems):
    count, lines, length = arrived.shape
    per = lines // (3 * depth)
    total = per * depth
    lanes = jnp.concatenate([arrived[s].astype(F32) for s in range(count)], 1)
    rest = lanes[total : 2 * total] * (math.log2(math.e) / math.sqrt(depth))
    key_rows = []
    for _ in range(3):
        key_rows.append(rest.astype(BF16).astype(F32))
        rest = rest - key_rows[-1]
    key_rows = jnp.concatenate(key_rows, 0).T.astype(BF16)
    values = [
        with_sum_row(lanes[2 * total + h * depth : 2 * total + (h + 1) * depth]) for h in range(per)
    ]
    block = 2 * length
    copies = [pltpu.make_async_copy(done.at[k], result.at[k], sems.at[k]) for k in range(count)]
    heads = []

    def score(item):
        begin, h = item
        queries = padded_rows(lanes[h * depth : (h + 1) * depth, begin : begin + block], h * depth, total)
        scores = dot(key_rows, jnp.concatenate([queries] * 3, 0).astype(BF16))
        return scores, jnp.max(scores, 0, keepdims=True)

    def finish(item, scores, highest):
        begin, h = item
        probs = jnp.exp2(scores - highest).astype(BF16)
        heads.append(attended(dot(values[h], probs), depth))
        if h == per - 1:
            both = jnp.concatenate(heads, 0).astype(BF16)
            heads.clear()
            for k in range(begin // length, (begin + block) // length):
                done[k] = both[:, k * length - begin : (k + 1) * length - begin]
                copies[k].start()

    ahead_of([(begin, h) for begin in range(0, count * length, block) for h in range(per)], score, finish, 4)
    for copy in copies:
        copy.wait()


def row_attention_kernel(count, queries, *refs):
    pairs = refs[:count]
    tokens, weight, bias, partial = refs[count:]
    stripes, half, length = queries.shape
    depth = half // HALF
    together = 2
    both, key_rows, lines, done = [], [], [], {}
    for a in range(stripes):
        both.append(jnp.concatenate([ref[a].astype(F32) for ref in pairs], 1))
        key_rows.append(both[a][:half].T.astype(BF16))
        lines.append(queries[a].astype(F32))

    def score(item):
        a, h = item
        wide = [
            padded_rows(lines[a][g * depth : (g + 1) * depth], g * depth, half)
            for g in range(h, h + together)
        ]
        scores = dot(key_rows[a], jnp.concatenate(wide, 1).astype(BF16))
        return scores, jnp.max(scores, 0, keepdims=True)

    def finish(item, scores, highest):
        a, h = item
        probs = weights_of(scores, highest, depth)
        for k in range(together):
            g = h + k
            values = with_sum_row(both[a][half + g * depth : half + (g + 1) * depth])
            done[a, g] = attended(dot(values, probs[:, k * length : (k + 1) * length]), depth)

    items = [(a, h) for a in range(stripes) for h in range(0, HALF, together)]
    ahead_of(items, score, finish, 2)
    for a in range(stripes):
        attention = jnp.concatenate([done[a, g] for g in range(HALF)], 0).T.astype(BF16)
        here = pl.ds(a * length, length)
        partial[here] = (
            tokens[here].astype(F32) + dot(attention, weight[:half]) + bias[...].reshape(1, 2 * half)
        )


def output_kernel(arrived, partial, weight, output):
    rows, cols, width = output.shape
    half = width // 2
    count = arrived.shape[0]
    across = cols // SPLIT
    down = rows // SPLIT
    square = SPLIT * SPLIT
    each = count // across
    blocks = {}
    for b in range(across):
        lines = jnp.concatenate([arrived[b * each + k].astype(F32) for k in range(each)], 0)
        mixed = dot(lines.T.astype(BF16), weight[half:])
        for a in range(down):
            here = pl.ds((a * across + b) * square, square)
            blocks[a, b] = (partial[here] + mixed[a * square : (a + 1) * square]).reshape(
                SPLIT, SPLIT, width
            )
    for a in range(down):
        output[a * SPLIT : (a + 1) * SPLIT] = jnp.concatenate(
            [blocks[a, b] for b in range(across)], 1
        ).astype(BF16)


def call(kernel, name, out_shape, args, flops, scratch=(), loose=()):
    several = isinstance(out_shape, tuple)
    spaces = [pl.ANY if k in loose else pltpu.VMEM for k in range(len(out_shape) if several else 1)]
    specs = tuple(pl.BlockSpec(memory_space=space) for space in spaces)
    moved = sum(x.size * x.dtype.itemsize for x in args)
    return pl.pallas_call(
        kernel,
        out_shape=out_shape,
        in_specs=vmem(len(args)),
        out_specs=specs if several else specs[0],
        scratch_shapes=scratch,
        compiler_params=params(),
        cost_estimate=pl.CostEstimate(flops=flops, bytes_accessed=moved, transcendentals=0),
        name=name,
    )(*args)


def shape(dims, dtype=BF16):
    return jax.ShapeDtypeStruct(dims, dtype)


def gathered(value, axis):
    count = lax.axis_size(axis)
    held = [value]
    for step in range(count - 1, 0, -1):
        pairs = [(k, k ^ step) for k in range(count)]
        held.append(lax.ppermute(value, axis, pairs))
    return held


def exchanged(value, axis):
    count = lax.axis_size(axis)
    lead = 5 * count // 8
    order = [lead] + [k for k in range(count) if k != lead]
    return lax.all_to_all(value, axis, 0, 0, axis_index_groups=[order], tiled=True)


def on_device(
    image,
    conv_weight,
    conv_bias,
    merge_gain,
    merge_shift,
    norm_gain,
    norm_shift,
    qkv_weight,
    proj_weight,
    proj_bias,
):
    in_rows, in_cols, channels = image.shape
    rows, cols = in_rows // 2, in_cols // 2
    width = conv_weight.shape[3]
    half = width // 2
    depth = width // HEADS
    row_count = lax.axis_size("row")
    col_count = lax.axis_size("col")
    down = [(k, (k + 1) % row_count) for k in range(row_count)]
    right = [(k, (k + 1) % col_count) for k in range(col_count)]
    diagonal = []
    for r in range(row_count):
        for c in range(col_count):
            target = (r, 0) if c == col_count - 1 else ((r + 1) % row_count, c + 1)
            diagonal.append((r * col_count + c, target[0] * col_count + target[1]))
    bottom = image[in_rows - 1]
    near = 2 * SPLIT
    tail = call(corner_kernel, "corner", shape((near, channels)), (bottom,), 10**10)
    side = call(edge_kernel, "edge", shape((in_rows, channels)), (image,), 10**5)
    upper = lax.ppermute(bottom, "row", down)
    left = lax.ppermute(side, "col", right)
    corner = lax.ppermute(tail, ("row", "col"), diagonal)
    pixel_parts = -(-channels // LANES)
    merged = call(
        own_kernel,
        "own_tile",
        shape((rows * cols, width), F32),
        (image, conv_weight),
        10**9,
        [pltpu.VMEM((pixel_parts, in_rows + 1, in_cols + SPLIT, LANES), F32)],
    )
    stripes, across = rows // SPLIT, cols // SPLIT
    per = across * HALF // row_count
    lanes = rows * SPLIT
    tokens, normed, chunks = call(
        merge_kernel,
        "merge",
        (
            shape((rows * cols, width)),
            shape((rows * cols, width)),
            shape((row_count, 3 * per * depth, lanes)),
        ),
        (
            merged,
            upper,
            left,
            corner,
            conv_weight,
            qkv_weight,
            conv_bias,
            merge_gain,
            merge_shift,
            norm_gain,
            norm_shift,
        ),
        5 * 10**8,
        [
            pltpu.VMEM((pixel_parts, 2, max(in_rows, in_cols) + SPLIT, LANES), F32),
            pltpu.VMEM((row_count, 3 * per * depth, lanes), BF16),
            pltpu.SemaphoreType.DMA((row_count,)),
        ],
        (2,),
    )
    arrived = exchanged(chunks, "row")
    queries, pairs = call(
        row_qkv_kernel,
        "row_qkv",
        (shape((stripes, half, cols * SPLIT)), shape((stripes, width, cols * SPLIT))),
        (normed, qkv_weight),
        3 * 10**8,
    )
    held = gathered(pairs, "col")
    result = call(
        lambda *refs: col_attention_kernel(depth, *refs),
        "col_attention",
        shape((row_count, per * depth, lanes)),
        (arrived,),
        2 * 10**9,
        [pltpu.VMEM((row_count, per * depth, lanes), BF16), pltpu.SemaphoreType.DMA((row_count,))],
        (0,),
    )
    back = exchanged(result, "row")
    partial = call(
        lambda *refs: row_attention_kernel(len(held), *refs),
        "row_attention",
        shape((rows * cols, width), F32),
        (queries, *held, tokens, proj_weight, proj_bias),
        2 * 10**9,
    )
    return call(
        output_kernel,
        "output",
        shape((rows, cols, width)),
        (back, partial, proj_weight),
        10**8,
    )


def solution(mesh):
    return jax.shard_map(
        on_device,
        mesh=mesh,
        in_specs=(P("row", "col", None), P(), P(), P(), P(), P(), P(), P(), P(), P()),
        out_specs=P("row", "col", None),
        check_vma=False,
    )
```

```python
import math

import jax
import jax.numpy as jnp
from jax import lax
from jax.experimental import pallas as pl
from jax.experimental.pallas import tpu as pltpu
from jax.sharding import PartitionSpec as P

HEADS = 16
SPLIT = 8
HALF = HEADS // 2
F32 = jnp.float32
BF16 = jnp.bfloat16
LANES = 128


def params():
    return pltpu.CompilerParams(vmem_limit_bytes=48 * 1024 * 1024)


def vmem(count):
    return [pl.BlockSpec(memory_space=pltpu.VMEM)] * count


def dot(left, right):
    return jnp.dot(left, right, preferred_element_type=F32)


def layer_norm(values, gain, shift):
    center = values - jnp.mean(values, -1, keepdims=True)
    spread = jnp.mean(center * center, -1, keepdims=True)
    return center * lax.rsqrt(spread + 1e-05) * gain + shift


def quadrants(rows, cols):
    return [(a, b) for a in range(rows // SPLIT) for b in range(cols // SPLIT)]


def lane_parts(channels):
    return [(k, k * LANES, min(LANES, channels - k * LANES)) for k in range(-(-channels // LANES))]


def every_second(ref, index, first, count, channels):
    return jnp.concatenate(
        [ref[(part, *index, pl.ds(first, count, stride=2))][:, :size] for part, _, size in lane_parts(channels)],
        1,
    )


def edge_kernel(image, side):
    near = 2 * SPLIT
    side[...] = image[:, image.shape[1] - near :].astype(F32)[:, near - 1].astype(BF16)


def corner_kernel(bottom, corner):
    corner[...] = bottom[bottom.shape[0] - corner.shape[0] :]


def own_kernel(image, weight, merged, pixels):
    in_rows, in_cols, channels = image.shape
    rows, cols = in_rows // 2, in_cols // 2
    first = SPLIT
    pixels[:, 0] = jnp.zeros(pixels.shape[:1] + pixels.shape[2:], F32)
    pixels[:, :, :first] = jnp.zeros(pixels.shape[:2] + (first, LANES), F32)
    for part, start, size in lane_parts(channels):
        pixels[part, pl.ds(1, in_rows), pl.ds(first, in_cols), pl.ds(0, size)] = image[
            :, :, pl.ds(start, size)
        ].astype(F32)
    total = jnp.zeros((rows * cols, merged.shape[1]), F32)
    for tap in range(3):
        lines = [
            every_second(pixels, (i,), first - 1 + tap, cols, channels).astype(BF16)
            for i in range(in_rows + 1)
        ]
        for tap_row in range(3):
            window = jnp.concatenate(lines[tap_row : tap_row + 2 * rows - 1 : 2], 0)
            total = total + dot(window, weight[tap_row, tap])
    merged[...] = total


def kept(value, axis):
    return jnp.where(lax.axis_index(axis) == 0, jnp.zeros(value.shape, F32), value.astype(F32))


def merge_kernel(
    merged, upper, left, corner, weight, qkv, bias, gain, shift, gain2, shift2, tokens, normed, chunks, edges, held_chunks, sems
):
    in_rows, channels = left.shape
    in_cols = 4 * merged.shape[0] // in_rows
    rows, cols = in_rows // 2, in_cols // 2
    width = weight.shape[3]
    depth = width // HEADS
    first = SPLIT
    row = lambda ref: ref[...].reshape(1, width)
    for part, start, size in lane_parts(channels):
        lanes, here = pl.ds(0, size), pl.ds(start, size)
        edges[part, 0, pl.ds(first, in_cols), lanes] = kept(upper[:, here], "row")
        edges[part, 0, pl.ds(first - 1, 1), lanes] = kept(kept(corner[:, here], "row")[corner.shape[0] - 1 :], "col")
        edges[part, 1, pl.ds(first, in_rows), lanes] = kept(left[:, here], "col")
        edges[part, 1, pl.ds(first - 1, 1), lanes] = jnp.zeros((1, size), F32)
    above = [every_second(edges, (0,), first - 1 + tap, cols, channels).astype(BF16) for tap in range(3)]
    aside = [every_second(edges, (1,), first - 1 + tap, rows, channels).astype(BF16) for tap in range(3)]
    corner = dot(jnp.concatenate([above[0], aside[0]], 0), weight[0, 0])
    top = corner[:cols] + dot(above[1], weight[0, 1]) + dot(above[2], weight[0, 2])
    near = corner[cols:] + dot(aside[1], weight[1, 0]) + dot(aside[2], weight[2, 0])
    grid = merged[...].reshape(rows, cols, width)
    grid = jnp.concatenate([grid[:1] + top.reshape(1, cols, width), grid[1:]], 0)
    begin = lax.broadcasted_iota(jnp.int32, (rows, SPLIT, width), 1) == 0
    grid = jnp.concatenate(
        [grid[:, :SPLIT] + jnp.where(begin, near.reshape(rows, 1, width), 0.0), grid[:, SPLIT:]], 1
    )
    grid = jnp.concatenate(
        [
            grid[a * SPLIT : (a + 1) * SPLIT, b * SPLIT : (b + 1) * SPLIT].reshape(SPLIT * SPLIT, width)
            for a, b in quadrants(rows, cols)
        ],
        0,
    )
    held = layer_norm(grid + row(bias), row(gain), row(shift)).astype(BF16)
    tokens[...] = held
    again = layer_norm(held.astype(F32), row(gain2), row(shift2)).astype(BF16)
    normed[...] = again
    across = cols // SPLIT
    count = chunks.shape[0]
    per = across * HALF // count
    square = SPLIT * SPLIT
    copies = [pltpu.make_async_copy(held_chunks.at[k], chunks.at[k], sems.at[k]) for k in range(count)]
    for b in range(across):
        mine = [
            again[(a * across + b) * square : (a * across + b + 1) * square] for a in range(rows // SPLIT)
        ]
        mine = jnp.concatenate(mine, 0)
        lines = []
        for kind in range(3):
            begin = kind * width + width // 2
            base = begin // LANES * LANES
            wide = dot(mine, qkv[:, base : (kind + 1) * width])
            lines.append(wide.T[begin - base :])
        for item in range(b * HALF, (b + 1) * HALF, per):
            low = (item - b * HALF) * depth
            held_chunks[item // per] = jnp.concatenate(
                [kind[low : low + per * depth] for kind in lines], 0
            ).astype(BF16)
            copies[item // per].start()
    for copy in copies:
        copy.wait()


def row_qkv_kernel(normed, qkv, queries, pairs):
    width = normed.shape[1]
    half = width // 2
    step = normed.shape[0] // queries.shape[0]
    for a in range(queries.shape[0]):
        mine = normed[a * step : (a + 1) * step]
        for kind in range(3):
            begin = kind * width
            end = begin + -(-half // LANES) * LANES
            lines = dot(mine, qkv[:, begin:end]).T[:half].astype(BF16)
            if kind == 0:
                queries[a] = lines
            else:
                pairs[a, (kind - 1) * half : kind * half] = lines


def padded_rows(values, start, total):
    size, lanes = values.shape
    pieces = []
    if start:
        pieces.append(jnp.zeros((start, lanes), F32))
    pieces.append(values)
    if total - start - size:
        pieces.append(jnp.zeros((total - start - size, lanes), F32))
    return jnp.concatenate(pieces, 0)


def with_sum_row(values):
    lanes = values.shape[1]
    return jnp.concatenate(
        [values, jnp.ones((1, lanes), F32), jnp.zeros((7, lanes), F32)], 0
    ).astype(BF16)


def weights_of(scores, highest, depth):
    return jnp.exp2((scores - highest) * (math.log2(math.e) / math.sqrt(depth))).astype(BF16)


def ahead_of(items, score, finish, ahead):
    waiting = [score(item) for item in items[:ahead]]
    for k, item in enumerate(items):
        if k + ahead < len(items):
            waiting.append(score(items[k + ahead]))
        finish(item, *waiting.pop(0))


def attended(mixed, depth):
    return mixed[:depth] / mixed[depth : depth + 1]


def col_attention_kernel(depth, arrived, result, done, sems):
    count, lines, length = arrived.shape
    per = lines // (3 * depth)
    total = per * depth
    lanes = jnp.concatenate([arrived[s].astype(F32) for s in range(count)], 1)
    rest = lanes[total : 2 * total] * (math.log2(math.e) / math.sqrt(depth))
    key_rows = []
    for _ in range(3):
        key_rows.append(rest.astype(BF16).astype(F32))
        rest = rest - key_rows[-1]
    key_rows = jnp.concatenate(key_rows, 0).T.astype(BF16)
    values = [
        with_sum_row(lanes[2 * total + h * depth : 2 * total + (h + 1) * depth]) for h in range(per)
    ]
    block = 2 * length
    copies = [pltpu.make_async_copy(done.at[k], result.at[k], sems.at[k]) for k in range(count)]
    heads = []

    def score(item):
        begin, h = item
        queries = padded_rows(lanes[h * depth : (h + 1) * depth, begin : begin + block], h * depth, total)
        scores = dot(key_rows, jnp.concatenate([queries] * 3, 0).astype(BF16))
        return scores, jnp.max(scores, 0, keepdims=True)

    def finish(item, scores, highest):
        begin, h = item
        probs = jnp.exp2(scores - highest).astype(BF16)
        heads.append(attended(dot(values[h], probs), depth))
        if h == per - 1:
            both = jnp.concatenate(heads, 0).astype(BF16)
            heads.clear()
            for k in range(begin // length, (begin + block) // length):
                done[k] = both[:, k * length - begin : (k + 1) * length - begin]
                copies[k].start()

    ahead_of([(begin, h) for begin in range(0, count * length, block) for h in range(per)], score, finish, 4)
    for copy in copies:
        copy.wait()


def row_attention_kernel(count, queries, *refs):
    pairs = refs[:count]
    tokens, weight, bias, partial = refs[count:]
    stripes, half, length = queries.shape
    depth = half // HALF
    together = 2
    both, key_rows, lines, done = [], [], [], {}
    for a in range(stripes):
        both.append(jnp.concatenate([ref[a].astype(F32) for ref in pairs], 1))
        key_rows.append(both[a][:half].T.astype(BF16))
        lines.append(queries[a].astype(F32))

    def score(item):
        a, h = item
        wide = [
            padded_rows(lines[a][g * depth : (g + 1) * depth], g * depth, half)
            for g in range(h, h + together)
        ]
        scores = dot(key_rows[a], jnp.concatenate(wide, 1).astype(BF16))
        return scores, jnp.max(scores, 0, keepdims=True)

    def finish(item, scores, highest):
        a, h = item
        probs = weights_of(scores, highest, depth)
        for k in range(together):
            g = h + k
            values = with_sum_row(both[a][half + g * depth : half + (g + 1) * depth])
            done[a, g] = attended(dot(values, probs[:, k * length : (k + 1) * length]), depth)

    items = [(a, h) for a in range(stripes) for h in range(0, HALF, together)]
    ahead_of(items, score, finish, 2)
    for a in range(stripes):
        attention = jnp.concatenate([done[a, g] for g in range(HALF)], 0).T.astype(BF16)
        here = pl.ds(a * length, length)
        partial[here] = (
            tokens[here].astype(F32) + dot(attention, weight[:half]) + bias[...].reshape(1, 2 * half)
        )


def output_kernel(arrived, partial, weight, output):
    rows, cols, width = output.shape
    half = width // 2
    count = arrived.shape[0]
    across = cols // SPLIT
    down = rows // SPLIT
    square = SPLIT * SPLIT
    each = count // across
    blocks = {}
    for b in range(across):
        lines = jnp.concatenate([arrived[b * each + k].astype(F32) for k in range(each)], 0)
        mixed = dot(lines.T.astype(BF16), weight[half:])
        for a in range(down):
            here = pl.ds((a * across + b) * square, square)
            blocks[a, b] = (partial[here] + mixed[a * square : (a + 1) * square]).reshape(
                SPLIT, SPLIT, width
            )
    for a in range(down):
        output[a * SPLIT : (a + 1) * SPLIT] = jnp.concatenate(
            [blocks[a, b] for b in range(across)], 1
        ).astype(BF16)


def call(kernel, name, out_shape, args, flops, scratch=(), loose=()):
    several = isinstance(out_shape, tuple)
    spaces = [pl.ANY if k in loose else pltpu.VMEM for k in range(len(out_shape) if several else 1)]
    specs = tuple(pl.BlockSpec(memory_space=space) for space in spaces)
    moved = sum(x.size * x.dtype.itemsize for x in args)
    return pl.pallas_call(
        kernel,
        out_shape=out_shape,
        in_specs=vmem(len(args)),
        out_specs=specs if several else specs[0],
        scratch_shapes=scratch,
        compiler_params=params(),
        cost_estimate=pl.CostEstimate(flops=flops, bytes_accessed=moved, transcendentals=0),
        name=name,
    )(*args)


def shape(dims, dtype=BF16):
    return jax.ShapeDtypeStruct(dims, dtype)


def gathered(value, axis):
    count = lax.axis_size(axis)
    held = [value]
    for step in range(count - 1, 0, -1):
        pairs = [(k, k ^ step) for k in range(count)]
        held.append(lax.ppermute(value, axis, pairs))
    return held


def exchanged(value, axis):
    count = lax.axis_size(axis)
    lead = count // 4
    order = [lead] + [k for k in range(count) if k != lead]
    return lax.all_to_all(value, axis, 0, 0, axis_index_groups=[order], tiled=True)


def on_device(
    image,
    conv_weight,
    conv_bias,
    merge_gain,
    merge_shift,
    norm_gain,
    norm_shift,
    qkv_weight,
    proj_weight,
    proj_bias,
):
    in_rows, in_cols, channels = image.shape
    rows, cols = in_rows // 2, in_cols // 2
    width = conv_weight.shape[3]
    half = width // 2
    depth = width // HEADS
    row_count = lax.axis_size("row")
    col_count = lax.axis_size("col")
    down = [(k, (k + 1) % row_count) for k in range(row_count)]
    right = [(k, (k + 1) % col_count) for k in range(col_count)]
    diagonal = []
    for r in range(row_count):
        for c in range(col_count):
            target = (r, 0) if c == col_count - 1 else ((r + 1) % row_count, c + 1)
            diagonal.append((r * col_count + c, target[0] * col_count + target[1]))
    bottom = image[in_rows - 1]
    near = 2 * SPLIT
    tail = call(corner_kernel, "corner", shape((near, channels)), (bottom,), 10**10)
    side = call(edge_kernel, "edge", shape((in_rows, channels)), (image,), 10**5)
    upper = lax.ppermute(bottom, "row", down)
    left = lax.ppermute(side, "col", right)
    corner = lax.ppermute(tail, ("row", "col"), diagonal)
    pixel_parts = -(-channels // LANES)
    merged = call(
        own_kernel,
        "own_tile",
        shape((rows * cols, width), F32),
        (image, conv_weight),
        10**9,
        [pltpu.VMEM((pixel_parts, in_rows + 1, in_cols + SPLIT, LANES), F32)],
    )
    stripes, across = rows // SPLIT, cols // SPLIT
    per = across * HALF // row_count
    lanes = rows * SPLIT
    tokens, normed, chunks = call(
        merge_kernel,
        "merge",
        (
            shape((rows * cols, width)),
            shape((rows * cols, width)),
            shape((row_count, 3 * per * depth, lanes)),
        ),
        (
            merged,
            upper,
            left,
            corner,
            conv_weight,
            qkv_weight,
            conv_bias,
            merge_gain,
            merge_shift,
            norm_gain,
            norm_shift,
        ),
        5 * 10**8,
        [
            pltpu.VMEM((pixel_parts, 2, max(in_rows, in_cols) + SPLIT, LANES), F32),
            pltpu.VMEM((row_count, 3 * per * depth, lanes), BF16),
            pltpu.SemaphoreType.DMA((row_count,)),
        ],
        (2,),
    )
    arrived = exchanged(chunks, "row")
    queries, pairs = call(
        row_qkv_kernel,
        "row_qkv",
        (shape((stripes, half, cols * SPLIT)), shape((stripes, width, cols * SPLIT))),
        (normed, qkv_weight),
        3 * 10**8,
    )
    held = gathered(pairs, "col")
    result = call(
        lambda *refs: col_attention_kernel(depth, *refs),
        "col_attention",
        shape((row_count, per * depth, lanes)),
        (arrived,),
        2 * 10**9,
        [pltpu.VMEM((row_count, per * depth, lanes), BF16), pltpu.SemaphoreType.DMA((row_count,))],
        (0,),
    )
    back = exchanged(result, "row")
    partial = call(
        lambda *refs: row_attention_kernel(len(held), *refs),
        "row_attention",
        shape((rows * cols, width), F32),
        (queries, *held, tokens, proj_weight, proj_bias),
        2 * 10**9,
    )
    return call(
        output_kernel,
        "output",
        shape((rows, cols, width)),
        (back, partial, proj_weight),
        10**8,
    )


def solution(mesh):
    return jax.shard_map(
        on_device,
        mesh=mesh,
        in_specs=(P("row", "col", None), P(), P(), P(), P(), P(), P(), P(), P(), P()),
        out_specs=P("row", "col", None),
        check_vma=False,
    )
```

```python
import math

import jax
import jax.numpy as jnp
from jax import lax
from jax.experimental import pallas as pl
from jax.experimental.pallas import tpu as pltpu
from jax.sharding import PartitionSpec as P

HEADS = 16
SPLIT = 8
HALF = HEADS // 2
F32 = jnp.float32
BF16 = jnp.bfloat16
LANES = 128


def params():
    return pltpu.CompilerParams(vmem_limit_bytes=48 * 1024 * 1024)


def vmem(count):
    return [pl.BlockSpec(memory_space=pltpu.VMEM)] * count


def dot(left, right):
    return jnp.dot(left, right, preferred_element_type=F32)


def layer_norm(values, gain, shift):
    center = values - jnp.mean(values, -1, keepdims=True)
    spread = jnp.mean(center * center, -1, keepdims=True)
    return center * lax.rsqrt(spread + 1e-05) * gain + shift


def quadrants(rows, cols):
    return [(a, b) for a in range(rows // SPLIT) for b in range(cols // SPLIT)]


def lane_parts(channels):
    return [(k, k * LANES, min(LANES, channels - k * LANES)) for k in range(-(-channels // LANES))]


def every_second(ref, index, first, count, channels):
    return jnp.concatenate(
        [ref[(part, *index, pl.ds(first, count, stride=2))][:, :size] for part, _, size in lane_parts(channels)],
        1,
    )


def edge_kernel(image, side):
    near = 2 * SPLIT
    side[...] = image[:, image.shape[1] - near :].astype(F32)[:, near - 1].astype(BF16)


def corner_kernel(bottom, corner):
    corner[...] = bottom[bottom.shape[0] - corner.shape[0] :]


def own_kernel(image, weight, merged, pixels):
    in_rows, in_cols, channels = image.shape
    rows, cols = in_rows // 2, in_cols // 2
    first = SPLIT
    pixels[:, 0] = jnp.zeros(pixels.shape[:1] + pixels.shape[2:], F32)
    pixels[:, :, :first] = jnp.zeros(pixels.shape[:2] + (first, LANES), F32)
    for part, start, size in lane_parts(channels):
        pixels[part, pl.ds(1, in_rows), pl.ds(first, in_cols), pl.ds(0, size)] = image[
            :, :, pl.ds(start, size)
        ].astype(F32)
    total = jnp.zeros((rows * cols, merged.shape[1]), F32)
    for tap in range(3):
        lines = [
            every_second(pixels, (i,), first - 1 + tap, cols, channels).astype(BF16)
            for i in range(in_rows + 1)
        ]
        for tap_row in range(3):
            window = jnp.concatenate(lines[tap_row : tap_row + 2 * rows - 1 : 2], 0)
            total = total + dot(window, weight[tap_row, tap])
    merged[...] = total


def kept(value, axis):
    return jnp.where(lax.axis_index(axis) == 0, jnp.zeros(value.shape, F32), value.astype(F32))


def merge_kernel(
    merged, upper, left, corner, weight, qkv, bias, gain, shift, gain2, shift2, tokens, normed, chunks, edges, held_chunks, sems
):
    in_rows, channels = left.shape
    in_cols = 4 * merged.shape[0] // in_rows
    rows, cols = in_rows // 2, in_cols // 2
    width = weight.shape[3]
    depth = width // HEADS
    first = SPLIT
    row = lambda ref: ref[...].reshape(1, width)
    for part, start, size in lane_parts(channels):
        lanes, here = pl.ds(0, size), pl.ds(start, size)
        edges[part, 0, pl.ds(first, in_cols), lanes] = kept(upper[:, here], "row")
        edges[part, 0, pl.ds(first - 1, 1), lanes] = kept(kept(corner[:, here], "row")[corner.shape[0] - 1 :], "col")
        edges[part, 1, pl.ds(first, in_rows), lanes] = kept(left[:, here], "col")
        edges[part, 1, pl.ds(first - 1, 1), lanes] = jnp.zeros((1, size), F32)
    above = [every_second(edges, (0,), first - 1 + tap, cols, channels).astype(BF16) for tap in range(3)]
    aside = [every_second(edges, (1,), first - 1 + tap, rows, channels).astype(BF16) for tap in range(3)]
    corner = dot(jnp.concatenate([above[0], aside[0]], 0), weight[0, 0])
    top = corner[:cols] + dot(above[1], weight[0, 1]) + dot(above[2], weight[0, 2])
    near = corner[cols:] + dot(aside[1], weight[1, 0]) + dot(aside[2], weight[2, 0])
    grid = merged[...].reshape(rows, cols, width)
    grid = jnp.concatenate([grid[:1] + top.reshape(1, cols, width), grid[1:]], 0)
    begin = lax.broadcasted_iota(jnp.int32, (rows, SPLIT, width), 1) == 0
    grid = jnp.concatenate(
        [grid[:, :SPLIT] + jnp.where(begin, near.reshape(rows, 1, width), 0.0), grid[:, SPLIT:]], 1
    )
    grid = jnp.concatenate(
        [
            grid[a * SPLIT : (a + 1) * SPLIT, b * SPLIT : (b + 1) * SPLIT].reshape(SPLIT * SPLIT, width)
            for a, b in quadrants(rows, cols)
        ],
        0,
    )
    held = layer_norm(grid + row(bias), row(gain), row(shift)).astype(BF16)
    tokens[...] = held
    again = layer_norm(held.astype(F32), row(gain2), row(shift2)).astype(BF16)
    normed[...] = again
    across = cols // SPLIT
    count = chunks.shape[0]
    per = across * HALF // count
    square = SPLIT * SPLIT
    copies = [pltpu.make_async_copy(held_chunks.at[k], chunks.at[k], sems.at[k]) for k in range(count)]
    for b in range(across):
        mine = [
            again[(a * across + b) * square : (a * across + b + 1) * square] for a in range(rows // SPLIT)
        ]
        mine = jnp.concatenate(mine, 0)
        lines = []
        for kind in range(3):
            begin = kind * width + width // 2
            base = begin // LANES * LANES
            wide = dot(mine, qkv[:, base : (kind + 1) * width])
            lines.append(wide.T[begin - base :])
        for item in range(b * HALF, (b + 1) * HALF, per):
            low = (item - b * HALF) * depth
            held_chunks[item // per] = jnp.concatenate(
                [kind[low : low + per * depth] for kind in lines], 0
            ).astype(BF16)
            copies[item // per].start()
    for copy in copies:
        copy.wait()


def row_qkv_kernel(normed, qkv, queries, pairs):
    width = normed.shape[1]
    half = width // 2
    step = normed.shape[0] // queries.shape[0]
    for a in range(queries.shape[0]):
        mine = normed[a * step : (a + 1) * step]
        for kind in range(3):
            begin = kind * width
            end = begin + -(-half // LANES) * LANES
            lines = dot(mine, qkv[:, begin:end]).T[:half].astype(BF16)
            if kind == 0:
                queries[a] = lines
            else:
                pairs[a, (kind - 1) * half : kind * half] = lines


def padded_rows(values, start, total):
    size, lanes = values.shape
    pieces = []
    if start:
        pieces.append(jnp.zeros((start, lanes), F32))
    pieces.append(values)
    if total - start - size:
        pieces.append(jnp.zeros((total - start - size, lanes), F32))
    return jnp.concatenate(pieces, 0)


def with_sum_row(values):
    lanes = values.shape[1]
    return jnp.concatenate(
        [values, jnp.ones((1, lanes), F32), jnp.zeros((7, lanes), F32)], 0
    ).astype(BF16)


def weights_of(scores, highest, depth):
    return jnp.exp2((scores - highest) * (math.log2(math.e) / math.sqrt(depth))).astype(BF16)


def ahead_of(items, score, finish, ahead):
    waiting = [score(item) for item in items[:ahead]]
    for k, item in enumerate(items):
        if k + ahead < len(items):
            waiting.append(score(items[k + ahead]))
        finish(item, *waiting.pop(0))


def attended(mixed, depth):
    return mixed[:depth] / mixed[depth : depth + 1]


def col_attention_kernel(depth, arrived, result, done, sems):
    count, lines, length = arrived.shape
    per = lines // (3 * depth)
    total = per * depth
    lanes = jnp.concatenate([arrived[s].astype(F32) for s in range(count)], 1)
    rest = lanes[total : 2 * total] * (math.log2(math.e) / math.sqrt(depth))
    key_rows = []
    for _ in range(3):
        key_rows.append(rest.astype(BF16).astype(F32))
        rest = rest - key_rows[-1]
    key_rows = jnp.concatenate(key_rows, 0).T.astype(BF16)
    values = [
        with_sum_row(lanes[2 * total + h * depth : 2 * total + (h + 1) * depth]) for h in range(per)
    ]
    block = 2 * length
    copies = [pltpu.make_async_copy(done.at[k], result.at[k], sems.at[k]) for k in range(count)]
    heads = []

    def score(item):
        begin, h = item
        queries = padded_rows(lanes[h * depth : (h + 1) * depth, begin : begin + block], h * depth, total)
        scores = dot(key_rows, jnp.concatenate([queries] * 3, 0).astype(BF16))
        return scores, jnp.max(scores, 0, keepdims=True)

    def finish(item, scores, highest):
        begin, h = item
        probs = jnp.exp2(scores - highest).astype(BF16)
        heads.append(attended(dot(values[h], probs), depth))
        if h == per - 1:
            both = jnp.concatenate(heads, 0).astype(BF16)
            heads.clear()
            for k in range(begin // length, (begin + block) // length):
                done[k] = both[:, k * length - begin : (k + 1) * length - begin]
                copies[k].start()

    ahead_of([(begin, h) for begin in range(0, count * length, block) for h in range(per)], score, finish, 4)
    for copy in copies:
        copy.wait()


def row_attention_kernel(count, queries, *refs):
    pairs = refs[:count]
    tokens, weight, bias, partial = refs[count:]
    stripes, half, length = queries.shape
    depth = half // HALF
    together = 2
    both, key_rows, lines, done = [], [], [], {}
    for a in range(stripes):
        both.append(jnp.concatenate([ref[a].astype(F32) for ref in pairs], 1))
        key_rows.append(both[a][:half].T.astype(BF16))
        lines.append(queries[a].astype(F32))

    def score(item):
        a, h = item
        wide = [
            padded_rows(lines[a][g * depth : (g + 1) * depth], g * depth, half)
            for g in range(h, h + together)
        ]
        scores = dot(key_rows[a], jnp.concatenate(wide, 1).astype(BF16))
        return scores, jnp.max(scores, 0, keepdims=True)

    def finish(item, scores, highest):
        a, h = item
        probs = weights_of(scores, highest, depth)
        for k in range(together):
            g = h + k
            values = with_sum_row(both[a][half + g * depth : half + (g + 1) * depth])
            done[a, g] = attended(dot(values, probs[:, k * length : (k + 1) * length]), depth)

    items = [(a, h) for a in range(stripes) for h in range(0, HALF, together)]
    ahead_of(items, score, finish, 2)
    for a in range(stripes):
        attention = jnp.concatenate([done[a, g] for g in range(HALF)], 0).T.astype(BF16)
        here = pl.ds(a * length, length)
        partial[here] = (
            tokens[here].astype(F32) + dot(attention, weight[:half]) + bias[...].reshape(1, 2 * half)
        )


def output_kernel(arrived, partial, weight, output):
    rows, cols, width = output.shape
    half = width // 2
    count = arrived.shape[0]
    across = cols // SPLIT
    down = rows // SPLIT
    square = SPLIT * SPLIT
    each = count // across
    blocks = {}
    for b in range(across):
        lines = jnp.concatenate([arrived[b * each + k].astype(F32) for k in range(each)], 0)
        mixed = dot(lines.T.astype(BF16), weight[half:])
        for a in range(down):
            here = pl.ds((a * across + b) * square, square)
            blocks[a, b] = (partial[here] + mixed[a * square : (a + 1) * square]).reshape(
                SPLIT, SPLIT, width
            )
    for a in range(down):
        output[a * SPLIT : (a + 1) * SPLIT] = jnp.concatenate(
            [blocks[a, b] for b in range(across)], 1
        ).astype(BF16)


def call(kernel, name, out_shape, args, flops, scratch=(), loose=()):
    several = isinstance(out_shape, tuple)
    spaces = [pl.ANY if k in loose else pltpu.VMEM for k in range(len(out_shape) if several else 1)]
    specs = tuple(pl.BlockSpec(memory_space=space) for space in spaces)
    moved = sum(x.size * x.dtype.itemsize for x in args)
    return pl.pallas_call(
        kernel,
        out_shape=out_shape,
        in_specs=vmem(len(args)),
        out_specs=specs if several else specs[0],
        scratch_shapes=scratch,
        compiler_params=params(),
        cost_estimate=pl.CostEstimate(flops=flops, bytes_accessed=moved, transcendentals=0),
        name=name,
    )(*args)


def shape(dims, dtype=BF16):
    return jax.ShapeDtypeStruct(dims, dtype)


def gathered(value, axis):
    count = lax.axis_size(axis)
    held = [value]
    for step in range(count - 1, 0, -1):
        pairs = [(k, k ^ step) for k in range(count)]
        held.append(lax.ppermute(value, axis, pairs))
    return held


def exchanged(value, axis):
    count = lax.axis_size(axis)
    lead = count // 4
    order = [lead] + [k for k in range(count) if k != lead]
    return lax.all_to_all(value, axis, 0, 0, axis_index_groups=[order], tiled=True)


def on_device(
    image,
    conv_weight,
    conv_bias,
    merge_gain,
    merge_shift,
    norm_gain,
    norm_shift,
    qkv_weight,
    proj_weight,
    proj_bias,
):
    in_rows, in_cols, channels = image.shape
    rows, cols = in_rows // 2, in_cols // 2
    width = conv_weight.shape[3]
    half = width // 2
    depth = width // HEADS
    row_count = lax.axis_size("row")
    col_count = lax.axis_size("col")
    down = [(k, (k + 1) % row_count) for k in range(row_count)]
    right = [(k, (k + 1) % col_count) for k in range(col_count)]
    diagonal = []
    for r in range(row_count):
        for c in range(col_count):
            target = (r, 0) if c == col_count - 1 else ((r + 1) % row_count, c + 1)
            diagonal.append((r * col_count + c, target[0] * col_count + target[1]))
    bottom = image[in_rows - 1]
    near = 2 * SPLIT
    tail = call(corner_kernel, "corner", shape((near, channels)), (bottom,), 10**10)
    side = call(edge_kernel, "edge", shape((in_rows, channels)), (image,), 10**5)
    upper = lax.ppermute(bottom, "row", down)
    left = lax.ppermute(side, "col", right)
    corner = lax.ppermute(tail, ("row", "col"), diagonal)
    pixel_parts = -(-channels // LANES)
    merged = call(
        own_kernel,
        "own_tile",
        shape((rows * cols, width), F32),
        (image, conv_weight),
        10**9,
        [pltpu.VMEM((pixel_parts, in_rows + 1, in_cols + 2 * SPLIT, LANES), F32)],
    )
    stripes, across = rows // SPLIT, cols // SPLIT
    per = across * HALF // row_count
    lanes = rows * SPLIT
    tokens, normed, chunks = call(
        merge_kernel,
        "merge",
        (
            shape((rows * cols, width)),
            shape((rows * cols, width)),
            shape((row_count, 3 * per * depth, lanes)),
        ),
        (
            merged,
            upper,
            left,
            corner,
            conv_weight,
            qkv_weight,
            conv_bias,
            merge_gain,
            merge_shift,
            norm_gain,
            norm_shift,
        ),
        5 * 10**8,
        [
            pltpu.VMEM((pixel_parts, 2, max(in_rows, in_cols) + 2 * SPLIT, LANES), F32),
            pltpu.VMEM((row_count, 3 * per * depth, lanes), BF16),
            pltpu.SemaphoreType.DMA((row_count,)),
        ],
        (2,),
    )
    arrived = exchanged(chunks, "row")
    queries, pairs = call(
        row_qkv_kernel,
        "row_qkv",
        (shape((stripes, half, cols * SPLIT)), shape((stripes, width, cols * SPLIT))),
        (normed, qkv_weight),
        3 * 10**8,
    )
    held = gathered(pairs, "col")
    result = call(
        lambda *refs: col_attention_kernel(depth, *refs),
        "col_attention",
        shape((row_count, per * depth, lanes)),
        (arrived,),
        2 * 10**9,
        [pltpu.VMEM((row_count, per * depth, lanes), BF16), pltpu.SemaphoreType.DMA((row_count,))],
        (0,),
    )
    back = exchanged(result, "row")
    partial = call(
        lambda *refs: row_attention_kernel(len(held), *refs),
        "row_attention",
        shape((rows * cols, width), F32),
        (queries, *held, tokens, proj_weight, proj_bias),
        2 * 10**9,
    )
    return call(
        output_kernel,
        "output",
        shape((rows, cols, width)),
        (back, partial, proj_weight),
        10**8,
    )


def solution(mesh):
    return jax.shard_map(
        on_device,
        mesh=mesh,
        in_specs=(P("row", "col", None), P(), P(), P(), P(), P(), P(), P(), P(), P()),
        out_specs=P("row", "col", None),
        check_vma=False,
    )
```

```python
import math

import jax
import jax.numpy as jnp
from jax import lax
from jax.experimental import pallas as pl
from jax.experimental.pallas import tpu as pltpu
from jax.sharding import PartitionSpec as P

HEADS = 16
SPLIT = 8
HALF = HEADS // 2
F32 = jnp.float32
BF16 = jnp.bfloat16
LANES = 128


def params():
    return pltpu.CompilerParams(vmem_limit_bytes=48 * 1024 * 1024)


def vmem(count):
    return [pl.BlockSpec(memory_space=pltpu.VMEM)] * count


def dot(left, right):
    return jnp.dot(left, right, preferred_element_type=F32)


def layer_norm(values, gain, shift):
    center = values - jnp.mean(values, -1, keepdims=True)
    spread = jnp.mean(center * center, -1, keepdims=True)
    return center * lax.rsqrt(spread + 1e-05) * gain + shift


def quadrants(rows, cols):
    return [(a, b) for a in range(rows // SPLIT) for b in range(cols // SPLIT)]


def lane_parts(channels):
    return [(k, k * LANES, min(LANES, channels - k * LANES)) for k in range(-(-channels // LANES))]


def every_second(ref, index, first, count, channels):
    return jnp.concatenate(
        [ref[(part, *index, pl.ds(first, count, stride=2))][:, :size] for part, _, size in lane_parts(channels)],
        1,
    )


def edge_kernel(image, side):
    near = 2 * SPLIT
    side[...] = image[:, image.shape[1] - near :].astype(F32)[:, near - 1].astype(BF16)


def corner_kernel(bottom, corner):
    corner[...] = bottom[bottom.shape[0] - corner.shape[0] :]


def own_kernel(
    image, weight, bias, gain, shift, gain2, shift2, near, top, tokens, normed, pixels
):
    in_rows, in_cols, channels = image.shape
    rows, cols = in_rows // 2, in_cols // 2
    first = SPLIT
    pixels[:, 0] = jnp.zeros(pixels.shape[:1] + pixels.shape[2:], F32)
    pixels[:, :, :first] = jnp.zeros(pixels.shape[:2] + (first, LANES), F32)
    for part, start, size in lane_parts(channels):
        pixels[part, pl.ds(1, in_rows), pl.ds(first, in_cols), pl.ds(0, size)] = image[
            :, :, pl.ds(start, size)
        ].astype(F32)
    width = weight.shape[3]
    total = jnp.zeros((rows * cols, width), F32)
    for tap in range(3):
        lines = [
            every_second(pixels, (i,), first - 1 + tap, cols, channels).astype(BF16)
            for i in range(in_rows + 1)
        ]
        for tap_row in range(3):
            window = jnp.concatenate(lines[tap_row : tap_row + 2 * rows - 1 : 2], 0)
            total = total + dot(window, weight[tap_row, tap])
    row = lambda ref: ref[...].reshape(1, width)
    total = (total + row(bias)).reshape(rows, cols, width)
    near[...] = total[:, :SPLIT]
    top[...] = total[0, SPLIT:]
    total = jnp.concatenate(
        [
            total[a * SPLIT : (a + 1) * SPLIT, b * SPLIT : (b + 1) * SPLIT].reshape(SPLIT * SPLIT, width)
            for a, b in quadrants(rows, cols)
            if b
        ],
        0,
    )
    held = layer_norm(total, row(gain), row(shift)).astype(BF16)
    tokens[...] = held
    normed[...] = layer_norm(held.astype(F32), row(gain2), row(shift2)).astype(BF16)


def kept(value, axis):
    return jnp.where(lax.axis_index(axis) == 0, jnp.zeros(value.shape, F32), value.astype(F32))


def merge_kernel(
    near_grid, own_top, own_tokens, own_normed, upper, left, corner, weight, qkv, gain, shift, gain2, shift2, tokens, normed, chunks, edges, held_chunks, sems
):
    in_rows, channels = left.shape
    in_cols = upper.shape[0]
    rows, cols = in_rows // 2, in_cols // 2
    width = weight.shape[3]
    depth = width // HEADS
    first = SPLIT
    row = lambda ref: ref[...].reshape(1, width)
    for part, start, size in lane_parts(channels):
        lanes, here = pl.ds(0, size), pl.ds(start, size)
        edges[part, 0, pl.ds(first, in_cols), lanes] = kept(upper[:, here], "row")
        edges[part, 0, pl.ds(first - 1, 1), lanes] = kept(kept(corner[:, here], "row")[corner.shape[0] - 1 :], "col")
        edges[part, 1, pl.ds(first, in_rows), lanes] = kept(left[:, here], "col")
        edges[part, 1, pl.ds(first - 1, 1), lanes] = jnp.zeros((1, size), F32)
    above = [every_second(edges, (0,), first - 1 + tap, cols, channels).astype(BF16) for tap in range(3)]
    aside = [every_second(edges, (1,), first - 1 + tap, rows, channels).astype(BF16) for tap in range(3)]
    corner = dot(jnp.concatenate([above[0], aside[0]], 0), weight[0, 0])
    top = corner[:cols] + dot(above[1], weight[0, 1]) + dot(above[2], weight[0, 2])
    near = corner[cols:] + dot(aside[1], weight[1, 0]) + dot(aside[2], weight[2, 0])
    grid = near_grid[...]
    grid = jnp.concatenate([grid[:1] + top[:SPLIT].reshape(1, SPLIT, width), grid[1:]], 0)
    begin = lax.broadcasted_iota(jnp.int32, (rows, SPLIT, width), 1) == 0
    grid = (grid + jnp.where(begin, near.reshape(rows, 1, width), 0.0)).reshape(rows * SPLIT, width)
    grid = jnp.concatenate([grid, own_top[...] + top[SPLIT:]], 0)
    square = SPLIT * SPLIT
    others = cols // SPLIT - 1

    def joined(mine, rest):
        pieces = []
        for a, b in quadrants(rows, cols):
            if b == 0:
                pieces.append(mine[a * square : (a + 1) * square])
                continue
            begin = (a * others + b - 1) * square
            piece = rest[begin : begin + square]
            if a == 0:
                first_row = rows * SPLIT + (b - 1) * SPLIT
                piece = jnp.concatenate([mine[first_row : first_row + SPLIT], piece[SPLIT:]], 0)
            pieces.append(piece)
        return jnp.concatenate(pieces, 0).astype(BF16)

    held = layer_norm(grid, row(gain), row(shift)).astype(BF16).astype(F32)
    tokens[...] = joined(held, own_tokens[...].astype(F32))
    again = joined(layer_norm(held, row(gain2), row(shift2)), own_normed[...].astype(F32))
    normed[...] = again
    across = cols // SPLIT
    count = chunks.shape[0]
    per = across * HALF // count
    square = SPLIT * SPLIT
    copies = [pltpu.make_async_copy(held_chunks.at[k], chunks.at[k], sems.at[k]) for k in range(count)]
    for b in range(across):
        mine = [
            again[(a * across + b) * square : (a * across + b + 1) * square] for a in range(rows // SPLIT)
        ]
        mine = jnp.concatenate(mine, 0)
        lines = []
        for kind in range(3):
            begin = kind * width + width // 2
            base = begin // LANES * LANES
            wide = dot(mine, qkv[:, base : (kind + 1) * width])
            lines.append(wide.T[begin - base :])
        for item in range(b * HALF, (b + 1) * HALF, per):
            low = (item - b * HALF) * depth
            held_chunks[item // per] = jnp.concatenate(
                [kind[low : low + per * depth] for kind in lines], 0
            ).astype(BF16)
            copies[item // per].start()
    for copy in copies:
        copy.wait()


def row_qkv_kernel(normed, qkv, queries, pairs):
    width = normed.shape[1]
    half = width // 2
    step = normed.shape[0] // queries.shape[0]
    for a in range(queries.shape[0]):
        mine = normed[a * step : (a + 1) * step]
        for kind in range(3):
            begin = kind * width
            end = begin + -(-half // LANES) * LANES
            lines = dot(mine, qkv[:, begin:end]).T[:half].astype(BF16)
            if kind == 0:
                queries[a] = lines
            else:
                pairs[a, (kind - 1) * half : kind * half] = lines


def padded_rows(values, start, total):
    size, lanes = values.shape
    pieces = []
    if start:
        pieces.append(jnp.zeros((start, lanes), F32))
    pieces.append(values)
    if total - start - size:
        pieces.append(jnp.zeros((total - start - size, lanes), F32))
    return jnp.concatenate(pieces, 0)


def with_sum_row(values):
    lanes = values.shape[1]
    return jnp.concatenate(
        [values, jnp.ones((1, lanes), F32), jnp.zeros((7, lanes), F32)], 0
    ).astype(BF16)


def weights_of(scores, highest, depth):
    return jnp.exp2((scores - highest) * (math.log2(math.e) / math.sqrt(depth))).astype(BF16)


def ahead_of(items, score, finish, ahead):
    waiting = [score(item) for item in items[:ahead]]
    for k, item in enumerate(items):
        if k + ahead < len(items):
            waiting.append(score(items[k + ahead]))
        finish(item, *waiting.pop(0))


def attended(mixed, depth):
    return mixed[:depth] / mixed[depth : depth + 1]


def col_attention_kernel(depth, arrived, result, done, sems):
    count, lines, length = arrived.shape
    per = lines // (3 * depth)
    total = per * depth
    lanes = jnp.concatenate([arrived[s].astype(F32) for s in range(count)], 1)
    rest = lanes[total : 2 * total] * (math.log2(math.e) / math.sqrt(depth))
    key_rows = []
    for _ in range(3):
        key_rows.append(rest.astype(BF16).astype(F32))
        rest = rest - key_rows[-1]
    key_rows = jnp.concatenate(key_rows, 0).T.astype(BF16)
    values = [
        with_sum_row(lanes[2 * total + h * depth : 2 * total + (h + 1) * depth]) for h in range(per)
    ]
    block = 2 * length
    copies = [pltpu.make_async_copy(done.at[k], result.at[k], sems.at[k]) for k in range(count)]
    heads = []

    def score(item):
        begin, h = item
        queries = padded_rows(lanes[h * depth : (h + 1) * depth, begin : begin + block], h * depth, total)
        scores = dot(key_rows, jnp.concatenate([queries] * 3, 0).astype(BF16))
        return scores, jnp.max(scores, 0, keepdims=True)

    def finish(item, scores, highest):
        begin, h = item
        probs = jnp.exp2(scores - highest).astype(BF16)
        heads.append(attended(dot(values[h], probs), depth))
        if h == per - 1:
            both = jnp.concatenate(heads, 0).astype(BF16)
            heads.clear()
            for k in range(begin // length, (begin + block) // length):
                done[k] = both[:, k * length - begin : (k + 1) * length - begin]
                copies[k].start()

    ahead_of([(begin, h) for begin in range(0, count * length, block) for h in range(per)], score, finish, 4)
    for copy in copies:
        copy.wait()


def row_attention_kernel(count, queries, *refs):
    pairs = refs[:count]
    tokens, weight, bias, partial = refs[count:]
    stripes, half, length = queries.shape
    depth = half // HALF
    together = 2
    both, key_rows, lines, done = [], [], [], {}
    for a in range(stripes):
        both.append(jnp.concatenate([ref[a].astype(F32) for ref in pairs], 1))
        key_rows.append(both[a][:half].T.astype(BF16))
        lines.append(queries[a].astype(F32))

    def score(item):
        a, h = item
        wide = [
            padded_rows(lines[a][g * depth : (g + 1) * depth], g * depth, half)
            for g in range(h, h + together)
        ]
        scores = dot(key_rows[a], jnp.concatenate(wide, 1).astype(BF16))
        return scores, jnp.max(scores, 0, keepdims=True)

    def finish(item, scores, highest):
        a, h = item
        probs = weights_of(scores, highest, depth)
        for k in range(together):
            g = h + k
            values = with_sum_row(both[a][half + g * depth : half + (g + 1) * depth])
            done[a, g] = attended(dot(values, probs[:, k * length : (k + 1) * length]), depth)

    items = [(a, h) for a in range(stripes) for h in range(0, HALF, together)]
    ahead_of(items, score, finish, 2)
    for a in range(stripes):
        attention = jnp.concatenate([done[a, g] for g in range(HALF)], 0).T.astype(BF16)
        here = pl.ds(a * length, length)
        partial[here] = (
            tokens[here].astype(F32) + dot(attention, weight[:half]) + bias[...].reshape(1, 2 * half)
        )


def output_kernel(arrived, partial, weight, output):
    rows, cols, width = output.shape
    half = width // 2
    count = arrived.shape[0]
    across = cols // SPLIT
    down = rows // SPLIT
    square = SPLIT * SPLIT
    each = count // across
    blocks = {}
    for b in range(across):
        lines = jnp.concatenate([arrived[b * each + k].astype(F32) for k in range(each)], 0)
        mixed = dot(lines.T.astype(BF16), weight[half:])
        for a in range(down):
            here = pl.ds((a * across + b) * square, square)
            blocks[a, b] = (partial[here] + mixed[a * square : (a + 1) * square]).reshape(
                SPLIT, SPLIT, width
            )
    for a in range(down):
        output[a * SPLIT : (a + 1) * SPLIT] = jnp.concatenate(
            [blocks[a, b] for b in range(across)], 1
        ).astype(BF16)


def call(kernel, name, out_shape, args, flops, scratch=(), loose=()):
    several = isinstance(out_shape, tuple)
    spaces = [pl.ANY if k in loose else pltpu.VMEM for k in range(len(out_shape) if several else 1)]
    specs = tuple(pl.BlockSpec(memory_space=space) for space in spaces)
    moved = sum(x.size * x.dtype.itemsize for x in args)
    return pl.pallas_call(
        kernel,
        out_shape=out_shape,
        in_specs=vmem(len(args)),
        out_specs=specs if several else specs[0],
        scratch_shapes=scratch,
        compiler_params=params(),
        cost_estimate=pl.CostEstimate(flops=flops, bytes_accessed=moved, transcendentals=0),
        name=name,
    )(*args)


def shape(dims, dtype=BF16):
    return jax.ShapeDtypeStruct(dims, dtype)


def gathered(value, axis):
    count = lax.axis_size(axis)
    held = [value]
    for step in range(count - 1, 0, -1):
        pairs = [(k, k ^ step) for k in range(count)]
        held.append(lax.ppermute(value, axis, pairs))
    return held


def exchanged(value, axis):
    count = lax.axis_size(axis)
    lead = count // 4
    order = [lead] + [k for k in range(count) if k != lead]
    return lax.all_to_all(value, axis, 0, 0, axis_index_groups=[order], tiled=True)


def on_device(
    image,
    conv_weight,
    conv_bias,
    merge_gain,
    merge_shift,
    norm_gain,
    norm_shift,
    qkv_weight,
    proj_weight,
    proj_bias,
):
    in_rows, in_cols, channels = image.shape
    rows, cols = in_rows // 2, in_cols // 2
    width = conv_weight.shape[3]
    half = width // 2
    depth = width // HEADS
    row_count = lax.axis_size("row")
    col_count = lax.axis_size("col")
    down = [(k, (k + 1) % row_count) for k in range(row_count)]
    right = [(k, (k + 1) % col_count) for k in range(col_count)]
    diagonal = []
    for r in range(row_count):
        for c in range(col_count):
            target = (r, 0) if c == col_count - 1 else ((r + 1) % row_count, c + 1)
            diagonal.append((r * col_count + c, target[0] * col_count + target[1]))
    bottom = image[in_rows - 1]
    near = 2 * SPLIT
    tail = call(corner_kernel, "corner", shape((near, channels)), (bottom,), 10**10)
    side = call(edge_kernel, "edge", shape((in_rows, channels)), (image,), 10**5)
    upper = lax.ppermute(bottom, "row", down)
    left = lax.ppermute(side, "col", right)
    corner = lax.ppermute(tail, ("row", "col"), diagonal)
    pixel_parts = -(-channels // LANES)
    norms = (merge_gain, merge_shift, norm_gain, norm_shift)
    apart = rows * (cols - SPLIT)
    own = call(
        own_kernel,
        "own_tile",
        (
            shape((rows, SPLIT, width), F32),
            shape((cols - SPLIT, width), F32),
            shape((apart, width)),
            shape((apart, width)),
        ),
        (image, conv_weight, conv_bias, *norms),
        10**9,
        [pltpu.VMEM((pixel_parts, in_rows + 1, in_cols + 2 * SPLIT, LANES), F32)],
    )
    stripes, across = rows // SPLIT, cols // SPLIT
    per = across * HALF // row_count
    lanes = rows * SPLIT
    tokens, normed, chunks = call(
        merge_kernel,
        "merge",
        (
            shape((rows * cols, width)),
            shape((rows * cols, width)),
            shape((row_count, 3 * per * depth, lanes)),
        ),
        (
            *own,
            upper,
            left,
            corner,
            conv_weight,
            qkv_weight,
            *norms,
        ),
        5 * 10**8,
        [
            pltpu.VMEM((pixel_parts, 2, max(in_rows, in_cols) + 2 * SPLIT, LANES), F32),
            pltpu.VMEM((row_count, 3 * per * depth, lanes), BF16),
            pltpu.SemaphoreType.DMA((row_count,)),
        ],
        (2,),
    )
    arrived = exchanged(chunks, "row")
    queries, pairs = call(
        row_qkv_kernel,
        "row_qkv",
        (shape((stripes, half, cols * SPLIT)), shape((stripes, width, cols * SPLIT))),
        (normed, qkv_weight),
        3 * 10**8,
    )
    held = gathered(pairs, "col")
    result = call(
        lambda *refs: col_attention_kernel(depth, *refs),
        "col_attention",
        shape((row_count, per * depth, lanes)),
        (arrived,),
        2 * 10**9,
        [pltpu.VMEM((row_count, per * depth, lanes), BF16), pltpu.SemaphoreType.DMA((row_count,))],
        (0,),
    )
    back = exchanged(result, "row")
    partial = call(
        lambda *refs: row_attention_kernel(len(held), *refs),
        "row_attention",
        shape((rows * cols, width), F32),
        (queries, *held, tokens, proj_weight, proj_bias),
        2 * 10**9,
    )
    return call(
        output_kernel,
        "output",
        shape((rows, cols, width)),
        (back, partial, proj_weight),
        10**8,
    )


def solution(mesh):
    return jax.shard_map(
        on_device,
        mesh=mesh,
        in_specs=(P("row", "col", None), P(), P(), P(), P(), P(), P(), P(), P(), P()),
        out_specs=P("row", "col", None),
        check_vma=False,
    )
```

```python
import math

import jax
import jax.numpy as jnp
from jax import lax
from jax.experimental import pallas as pl
from jax.experimental.pallas import tpu as pltpu
from jax.sharding import PartitionSpec as P

HEADS = 16
SPLIT = 8
HALF = HEADS // 2
F32 = jnp.float32
BF16 = jnp.bfloat16
LANES = 128


def params():
    return pltpu.CompilerParams(vmem_limit_bytes=48 * 1024 * 1024)


def vmem(count):
    return [pl.BlockSpec(memory_space=pltpu.VMEM)] * count


def dot(left, right):
    return jnp.dot(left, right, preferred_element_type=F32)


def layer_norm(values, gain, shift):
    center = values - jnp.mean(values, -1, keepdims=True)
    spread = jnp.mean(center * center, -1, keepdims=True)
    return center * lax.rsqrt(spread + 1e-05) * gain + shift


def quadrants(rows, cols):
    return [(a, b) for a in range(rows // SPLIT) for b in range(cols // SPLIT)]


def lane_parts(channels):
    return [(k, k * LANES, min(LANES, channels - k * LANES)) for k in range(-(-channels // LANES))]


def every_second(ref, index, first, count, channels):
    return jnp.concatenate(
        [ref[(part, *index, pl.ds(first, count, stride=2))][:, :size] for part, _, size in lane_parts(channels)],
        1,
    )


def edge_kernel(image, side):
    near = 2 * SPLIT
    side[...] = image[:, image.shape[1] - near :].astype(F32)[:, near - 1].astype(BF16)


def corner_kernel(bottom, corner):
    corner[...] = bottom[bottom.shape[0] - corner.shape[0] :]


def own_kernel(image, weight, merged, pixels):
    in_rows, in_cols, channels = image.shape
    rows, cols = in_rows // 2, in_cols // 2
    first = SPLIT
    pixels[:, 0] = jnp.zeros(pixels.shape[:1] + pixels.shape[2:], F32)
    pixels[:, :, :first] = jnp.zeros(pixels.shape[:2] + (first, LANES), F32)
    for part, start, size in lane_parts(channels):
        pixels[part, pl.ds(1, in_rows), pl.ds(first, in_cols), pl.ds(0, size)] = image[
            :, :, pl.ds(start, size)
        ].astype(F32)
    total = jnp.zeros((rows * cols, merged.shape[1]), F32)
    for tap in range(3):
        lines = [
            every_second(pixels, (i,), first - 1 + tap, cols, channels).astype(BF16)
            for i in range(in_rows + 1)
        ]
        for tap_row in range(3):
            window = jnp.concatenate(lines[tap_row : tap_row + 2 * rows - 1 : 2], 0)
            total = total + dot(window, weight[tap_row, tap])
    merged[...] = total


def kept(value, axis):
    return jnp.where(lax.axis_index(axis) == 0, jnp.zeros(value.shape, F32), value.astype(F32))


def merge_kernel(
    merged, upper, left, corner, weight, qkv, bias, gain, shift, gain2, shift2, tokens, normed, chunks, edges, held_chunks, sems
):
    in_rows, channels = left.shape
    in_cols = 4 * merged.shape[0] // in_rows
    rows, cols = in_rows // 2, in_cols // 2
    width = weight.shape[3]
    depth = width // HEADS
    first = SPLIT
    row = lambda ref: ref[...].reshape(1, width)
    for part, start, size in lane_parts(channels):
        lanes, here = pl.ds(0, size), pl.ds(start, size)
        edges[part, 0, pl.ds(first, in_cols), lanes] = kept(upper[:, here], "row")
        edges[part, 0, pl.ds(first - 1, 1), lanes] = kept(kept(corner[:, here], "row")[corner.shape[0] - 1 :], "col")
        edges[part, 1, pl.ds(first, in_rows), lanes] = kept(left[:, here], "col")
        edges[part, 1, pl.ds(first - 1, 1), lanes] = jnp.zeros((1, size), F32)
    above = [every_second(edges, (0,), first - 1 + tap, cols, channels).astype(BF16) for tap in range(3)]
    aside = [every_second(edges, (1,), first - 1 + tap, rows, channels).astype(BF16) for tap in range(3)]
    corner = dot(jnp.concatenate([above[0], aside[0]], 0), weight[0, 0])
    top = corner[:cols] + dot(above[1], weight[0, 1]) + dot(above[2], weight[0, 2])
    near = corner[cols:] + dot(aside[1], weight[1, 0]) + dot(aside[2], weight[2, 0])
    grid = merged[...].reshape(rows, cols, width)
    grid = jnp.concatenate([grid[:1] + top.reshape(1, cols, width), grid[1:]], 0)
    begin = lax.broadcasted_iota(jnp.int32, (rows, SPLIT, width), 1) == 0
    grid = jnp.concatenate(
        [grid[:, :SPLIT] + jnp.where(begin, near.reshape(rows, 1, width), 0.0), grid[:, SPLIT:]], 1
    )
    grid = jnp.concatenate(
        [
            grid[a * SPLIT : (a + 1) * SPLIT, b * SPLIT : (b + 1) * SPLIT].reshape(SPLIT * SPLIT, width)
            for a, b in quadrants(rows, cols)
        ],
        0,
    )
    held = layer_norm(grid + row(bias), row(gain), row(shift)).astype(BF16)
    tokens[...] = held
    again = layer_norm(held.astype(F32), row(gain2), row(shift2)).astype(BF16)
    normed[...] = again
    across = cols // SPLIT
    count = chunks.shape[0]
    per = across * HALF // count
    square = SPLIT * SPLIT
    copies = [pltpu.make_async_copy(held_chunks.at[k], chunks.at[k], sems.at[k]) for k in range(count)]
    mine = jnp.concatenate(
        [
            again[(a * across + b) * square : (a * across + b + 1) * square]
            for b in range(across)
            for a in range(rows // SPLIT)
        ],
        0,
    )
    turned = []
    for kind in range(3):
        begin = kind * width + width // 2
        base = begin // LANES * LANES
        wide = dot(mine, qkv[:, base : (kind + 1) * width])
        turned.append(wide.T[begin - base :])
    length = rows * SPLIT
    for b in range(across):
        lines = [kind[:, b * length : (b + 1) * length] for kind in turned]
        for item in range(b * HALF, (b + 1) * HALF, per):
            low = (item - b * HALF) * depth
            held_chunks[item // per] = jnp.concatenate(
                [kind[low : low + per * depth] for kind in lines], 0
            ).astype(BF16)
            copies[item // per].start()
    for copy in copies:
        copy.wait()


def row_qkv_kernel(normed, qkv, queries, pairs):
    width = normed.shape[1]
    half = width // 2
    step = normed.shape[0] // queries.shape[0]
    for a in range(queries.shape[0]):
        mine = normed[a * step : (a + 1) * step]
        for kind in range(3):
            begin = kind * width
            end = begin + -(-half // LANES) * LANES
            lines = dot(mine, qkv[:, begin:end]).T[:half].astype(BF16)
            if kind == 0:
                queries[a] = lines
            else:
                pairs[a, (kind - 1) * half : kind * half] = lines


def padded_rows(values, start, total):
    size, lanes = values.shape
    pieces = []
    if start:
        pieces.append(jnp.zeros((start, lanes), F32))
    pieces.append(values)
    if total - start - size:
        pieces.append(jnp.zeros((total - start - size, lanes), F32))
    return jnp.concatenate(pieces, 0)


def with_sum_row(values):
    lanes = values.shape[1]
    return jnp.concatenate(
        [values, jnp.ones((1, lanes), F32), jnp.zeros((7, lanes), F32)], 0
    ).astype(BF16)


def weights_of(scores, highest, depth):
    return jnp.exp2((scores - highest) * (math.log2(math.e) / math.sqrt(depth))).astype(BF16)


def ahead_of(items, score, finish, ahead):
    waiting = [score(item) for item in items[:ahead]]
    for k, item in enumerate(items):
        if k + ahead < len(items):
            waiting.append(score(items[k + ahead]))
        finish(item, *waiting.pop(0))


def attended(mixed, depth):
    return mixed[:depth] / mixed[depth : depth + 1]


def col_attention_kernel(depth, arrived, result, done, sems):
    count, lines, length = arrived.shape
    per = lines // (3 * depth)
    total = per * depth
    lanes = jnp.concatenate([arrived[s].astype(F32) for s in range(count)], 1)
    rest = lanes[total : 2 * total] * (math.log2(math.e) / math.sqrt(depth))
    key_rows = []
    for _ in range(3):
        key_rows.append(rest.astype(BF16).astype(F32))
        rest = rest - key_rows[-1]
    key_rows = jnp.concatenate(key_rows, 0).T.astype(BF16)
    values = [
        with_sum_row(lanes[2 * total + h * depth : 2 * total + (h + 1) * depth]) for h in range(per)
    ]
    block = 2 * length
    copies = [pltpu.make_async_copy(done.at[k], result.at[k], sems.at[k]) for k in range(count)]
    heads = []

    def score(item):
        begin, h = item
        queries = padded_rows(lanes[h * depth : (h + 1) * depth, begin : begin + block], h * depth, total)
        scores = dot(key_rows, jnp.concatenate([queries] * 3, 0).astype(BF16))
        return scores, jnp.max(scores, 0, keepdims=True)

    def finish(item, scores, highest):
        begin, h = item
        probs = jnp.exp2(scores - highest).astype(BF16)
        heads.append(attended(dot(values[h], probs), depth))
        if h == per - 1:
            both = jnp.concatenate(heads, 0).astype(BF16)
            heads.clear()
            for k in range(begin // length, (begin + block) // length):
                done[k] = both[:, k * length - begin : (k + 1) * length - begin]
                copies[k].start()

    ahead_of([(begin, h) for begin in range(0, count * length, block) for h in range(per)], score, finish, 6)
    for copy in copies:
        copy.wait()


def row_attention_kernel(count, queries, *refs):
    pairs = refs[:count]
    tokens, weight, bias, partial = refs[count:]
    stripes, half, length = queries.shape
    depth = half // HALF
    together = 2
    both, key_rows, lines, done = [], [], [], {}
    for a in range(stripes):
        both.append(jnp.concatenate([ref[a].astype(F32) for ref in pairs], 1))
        key_rows.append(both[a][:half].T.astype(BF16))
        lines.append(queries[a].astype(F32))

    def score(item):
        a, h = item
        wide = [
            padded_rows(lines[a][g * depth : (g + 1) * depth], g * depth, half)
            for g in range(h, h + together)
        ]
        scores = dot(key_rows[a], jnp.concatenate(wide, 1).astype(BF16))
        return scores, jnp.max(scores, 0, keepdims=True)

    def finish(item, scores, highest):
        a, h = item
        probs = weights_of(scores, highest, depth)
        for k in range(together):
            g = h + k
            values = with_sum_row(both[a][half + g * depth : half + (g + 1) * depth])
            done[a, g] = attended(dot(values, probs[:, k * length : (k + 1) * length]), depth)

    items = [(a, h) for a in range(stripes) for h in range(0, HALF, together)]
    ahead_of(items, score, finish, 2)
    for a in range(stripes):
        attention = jnp.concatenate([done[a, g] for g in range(HALF)], 0).T.astype(BF16)
        here = pl.ds(a * length, length)
        partial[here] = (
            tokens[here].astype(F32) + dot(attention, weight[:half]) + bias[...].reshape(1, 2 * half)
        )


def output_kernel(arrived, partial, weight, output):
    rows, cols, width = output.shape
    half = width // 2
    count = arrived.shape[0]
    across = cols // SPLIT
    down = rows // SPLIT
    square = SPLIT * SPLIT
    each = count // across
    blocks = {}
    lines = [
        jnp.concatenate([arrived[b * each + k].astype(F32) for k in range(each)], 0) for b in range(across)
    ]
    mixed = dot(jnp.concatenate(lines, 1).T.astype(BF16), weight[half:])
    for b in range(across):
        for a in range(down):
            here = pl.ds((a * across + b) * square, square)
            begin = (b * down + a) * square
            blocks[a, b] = (partial[here] + mixed[begin : begin + square]).reshape(SPLIT, SPLIT, width)
    for a in range(down):
        output[a * SPLIT : (a + 1) * SPLIT] = jnp.concatenate(
            [blocks[a, b] for b in range(across)], 1
        ).astype(BF16)


def call(kernel, name, out_shape, args, flops, scratch=(), loose=()):
    several = isinstance(out_shape, tuple)
    spaces = [pl.ANY if k in loose else pltpu.VMEM for k in range(len(out_shape) if several else 1)]
    specs = tuple(pl.BlockSpec(memory_space=space) for space in spaces)
    moved = sum(x.size * x.dtype.itemsize for x in args)
    return pl.pallas_call(
        kernel,
        out_shape=out_shape,
        in_specs=vmem(len(args)),
        out_specs=specs if several else specs[0],
        scratch_shapes=scratch,
        compiler_params=params(),
        cost_estimate=pl.CostEstimate(flops=flops, bytes_accessed=moved, transcendentals=0),
        name=name,
    )(*args)


def shape(dims, dtype=BF16):
    return jax.ShapeDtypeStruct(dims, dtype)


def gathered(value, axis):
    count = lax.axis_size(axis)
    held = [value]
    for step in range(count - 1, 0, -1):
        pairs = [(k, k ^ step) for k in range(count)]
        held.append(lax.ppermute(value, axis, pairs))
    return held


def exchanged(value, axis):
    count = lax.axis_size(axis)
    lead = count // 4
    order = [lead] + [k for k in range(count) if k != lead]
    return lax.all_to_all(value, axis, 0, 0, axis_index_groups=[order], tiled=True)


def on_device(
    image,
    conv_weight,
    conv_bias,
    merge_gain,
    merge_shift,
    norm_gain,
    norm_shift,
    qkv_weight,
    proj_weight,
    proj_bias,
):
    in_rows, in_cols, channels = image.shape
    rows, cols = in_rows // 2, in_cols // 2
    width = conv_weight.shape[3]
    half = width // 2
    depth = width // HEADS
    row_count = lax.axis_size("row")
    col_count = lax.axis_size("col")
    down = [(k, (k + 1) % row_count) for k in range(row_count)]
    right = [(k, (k + 1) % col_count) for k in range(col_count)]
    diagonal = []
    for r in range(row_count):
        for c in range(col_count):
            target = (r, 0) if c == col_count - 1 else ((r + 1) % row_count, c + 1)
            diagonal.append((r * col_count + c, target[0] * col_count + target[1]))
    bottom = image[in_rows - 1]
    near = 2 * SPLIT
    tail = call(corner_kernel, "corner", shape((near, channels)), (bottom,), 10**10)
    side = call(edge_kernel, "edge", shape((in_rows, channels)), (image,), 10**5)
    upper = lax.ppermute(bottom, "row", down)
    left = lax.ppermute(side, "col", right)
    corner = lax.ppermute(tail, ("row", "col"), diagonal)
    pixel_parts = -(-channels // LANES)
    merged = call(
        own_kernel,
        "own_tile",
        shape((rows * cols, width), F32),
        (image, conv_weight),
        10**9,
        [pltpu.VMEM((pixel_parts, in_rows + 1, in_cols + 2 * SPLIT, LANES), F32)],
    )
    stripes, across = rows // SPLIT, cols // SPLIT
    per = across * HALF // row_count
    lanes = rows * SPLIT
    tokens, normed, chunks = call(
        merge_kernel,
        "merge",
        (
            shape((rows * cols, width)),
            shape((rows * cols, width)),
            shape((row_count, 3 * per * depth, lanes)),
        ),
        (
            merged,
            upper,
            left,
            corner,
            conv_weight,
            qkv_weight,
            conv_bias,
            merge_gain,
            merge_shift,
            norm_gain,
            norm_shift,
        ),
        5 * 10**8,
        [
            pltpu.VMEM((pixel_parts, 2, max(in_rows, in_cols) + 2 * SPLIT, LANES), F32),
            pltpu.VMEM((row_count, 3 * per * depth, lanes), BF16),
            pltpu.SemaphoreType.DMA((row_count,)),
        ],
        (2,),
    )
    arrived = exchanged(chunks, "row")
    queries, pairs = call(
        row_qkv_kernel,
        "row_qkv",
        (shape((stripes, half, cols * SPLIT)), shape((stripes, width, cols * SPLIT))),
        (normed, qkv_weight),
        3 * 10**8,
    )
    held = gathered(pairs, "col")
    result = call(
        lambda *refs: col_attention_kernel(depth, *refs),
        "col_attention",
        shape((row_count, per * depth, lanes)),
        (arrived,),
        2 * 10**9,
        [pltpu.VMEM((row_count, per * depth, lanes), BF16), pltpu.SemaphoreType.DMA((row_count,))],
        (0,),
    )
    back = exchanged(result, "row")
    partial = call(
        lambda *refs: row_attention_kernel(len(held), *refs),
        "row_attention",
        shape((rows * cols, width), F32),
        (queries, *held, tokens, proj_weight, proj_bias),
        2 * 10**9,
    )
    return call(
        output_kernel,
        "output",
        shape((rows, cols, width)),
        (back, partial, proj_weight),
        10**8,
    )


def solution(mesh):
    return jax.shard_map(
        on_device,
        mesh=mesh,
        in_specs=(P("row", "col", None), P(), P(), P(), P(), P(), P(), P(), P(), P()),
        out_specs=P("row", "col", None),
        check_vma=False,
    )
```

```python
import math

import jax
import jax.numpy as jnp
from jax import lax
from jax.experimental import pallas as pl
from jax.experimental.pallas import tpu as pltpu
from jax.sharding import PartitionSpec as P

HEADS = 16
SPLIT = 8
HALF = HEADS // 2
F32 = jnp.float32
BF16 = jnp.bfloat16
LANES = 128


def params():
    return pltpu.CompilerParams(vmem_limit_bytes=48 * 1024 * 1024)


def vmem(count):
    return [pl.BlockSpec(memory_space=pltpu.VMEM)] * count


def dot(left, right):
    return jnp.dot(left, right, preferred_element_type=F32)


def layer_norm(values, gain, shift):
    center = values - jnp.mean(values, -1, keepdims=True)
    spread = jnp.mean(center * center, -1, keepdims=True)
    return center * lax.rsqrt(spread + 1e-05) * gain + shift


def quadrants(rows, cols):
    return [(a, b) for a in range(rows // SPLIT) for b in range(cols // SPLIT)]


def lane_parts(channels):
    return [(k, k * LANES, min(LANES, channels - k * LANES)) for k in range(-(-channels // LANES))]


def every_second(ref, index, first, count, channels):
    return jnp.concatenate(
        [ref[(part, *index, pl.ds(first, count, stride=2))][:, :size] for part, _, size in lane_parts(channels)],
        1,
    )


def edge_kernel(image, side):
    near = 2 * SPLIT
    side[...] = image[:, image.shape[1] - near :].astype(F32)[:, near - 1].astype(BF16)


def corner_kernel(bottom, corner):
    corner[...] = bottom[bottom.shape[0] - corner.shape[0] :]


def own_kernel(image, weight, merged, pixels):
    in_rows, in_cols, channels = image.shape
    rows, cols = in_rows // 2, in_cols // 2
    first = SPLIT
    pixels[:, 0] = jnp.zeros(pixels.shape[:1] + pixels.shape[2:], F32)
    pixels[:, :, :first] = jnp.zeros(pixels.shape[:2] + (first, LANES), F32)
    for part, start, size in lane_parts(channels):
        pixels[part, pl.ds(1, in_rows), pl.ds(first, in_cols), pl.ds(0, size)] = image[
            :, :, pl.ds(start, size)
        ].astype(F32)
    total = jnp.zeros((rows * cols, merged.shape[1]), F32)
    for tap in range(3):
        lines = [
            every_second(pixels, (i,), first - 1 + tap, cols, channels).astype(BF16)
            for i in range(in_rows + 1)
        ]
        for tap_row in range(3):
            window = jnp.concatenate(lines[tap_row : tap_row + 2 * rows - 1 : 2], 0)
            total = total + dot(window, weight[tap_row, tap])
    merged[...] = total


def kept(value, axis):
    return jnp.where(lax.axis_index(axis) == 0, jnp.zeros(value.shape, F32), value.astype(F32))


def merge_kernel(
    merged, upper, left, corner, weight, qkv, bias, gain, shift, gain2, shift2, tokens, normed, chunks, edges, held_chunks, sems
):
    in_rows, channels = left.shape
    in_cols = 4 * merged.shape[0] // in_rows
    rows, cols = in_rows // 2, in_cols // 2
    width = weight.shape[3]
    depth = width // HEADS
    first = SPLIT
    row = lambda ref: ref[...].reshape(1, width)
    for part, start, size in lane_parts(channels):
        lanes, here = pl.ds(0, size), pl.ds(start, size)
        edges[part, 0, pl.ds(first, in_cols), lanes] = kept(upper[:, here], "row")
        edges[part, 0, pl.ds(first - 1, 1), lanes] = kept(kept(corner[:, here], "row")[corner.shape[0] - 1 :], "col")
        edges[part, 1, pl.ds(first, in_rows), lanes] = kept(left[:, here], "col")
        edges[part, 1, pl.ds(first - 1, 1), lanes] = jnp.zeros((1, size), F32)
    above = [every_second(edges, (0,), first - 1 + tap, cols, channels).astype(BF16) for tap in range(3)]
    aside = [every_second(edges, (1,), first - 1 + tap, rows, channels).astype(BF16) for tap in range(3)]
    corner = dot(jnp.concatenate([above[0], aside[0]], 0), weight[0, 0])
    top = corner[:cols] + dot(above[1], weight[0, 1]) + dot(above[2], weight[0, 2])
    near = corner[cols:] + dot(aside[1], weight[1, 0]) + dot(aside[2], weight[2, 0])
    grid = merged[...].reshape(rows, cols, width)
    grid = jnp.concatenate([grid[:1] + top.reshape(1, cols, width), grid[1:]], 0)
    begin = lax.broadcasted_iota(jnp.int32, (rows, SPLIT, width), 1) == 0
    grid = jnp.concatenate(
        [grid[:, :SPLIT] + jnp.where(begin, near.reshape(rows, 1, width), 0.0), grid[:, SPLIT:]], 1
    )
    grid = jnp.concatenate(
        [
            grid[a * SPLIT : (a + 1) * SPLIT, b * SPLIT : (b + 1) * SPLIT].reshape(SPLIT * SPLIT, width)
            for a, b in quadrants(rows, cols)
        ],
        0,
    )
    held = layer_norm(grid + row(bias), row(gain), row(shift)).astype(BF16)
    tokens[...] = held
    again = layer_norm(held.astype(F32), row(gain2), row(shift2)).astype(BF16)
    normed[...] = again
    across = cols // SPLIT
    count = chunks.shape[0]
    per = across * HALF // count
    square = SPLIT * SPLIT
    copies = [pltpu.make_async_copy(held_chunks.at[k], chunks.at[k], sems.at[k]) for k in range(count)]
    for b in range(across):
        mine = [
            again[(a * across + b) * square : (a * across + b + 1) * square] for a in range(rows // SPLIT)
        ]
        mine = jnp.concatenate(mine, 0)
        lines = []
        for kind in range(3):
            begin = kind * width + width // 2
            base = begin // LANES * LANES
            wide = dot(mine, qkv[:, base : (kind + 1) * width])
            lines.append(wide.T[begin - base :])
        for item in range(b * HALF, (b + 1) * HALF, per):
            low = (item - b * HALF) * depth
            held_chunks[item // per] = jnp.concatenate(
                [kind[low : low + per * depth] for kind in lines], 0
            ).astype(BF16)
            copies[item // per].start()
    for copy in copies:
        copy.wait()


def row_qkv_kernel(normed, qkv, queries, pairs):
    width = normed.shape[1]
    half = width // 2
    step = normed.shape[0] // queries.shape[0]
    for a in range(queries.shape[0]):
        mine = normed[a * step : (a + 1) * step]
        for kind in range(3):
            begin = kind * width
            end = begin + -(-half // LANES) * LANES
            lines = dot(mine, qkv[:, begin:end]).T[:half].astype(BF16)
            if kind == 0:
                queries[a] = lines
            else:
                pairs[a, (kind - 1) * half : kind * half] = lines


def padded_rows(values, start, total):
    size, lanes = values.shape
    pieces = []
    if start:
        pieces.append(jnp.zeros((start, lanes), F32))
    pieces.append(values)
    if total - start - size:
        pieces.append(jnp.zeros((total - start - size, lanes), F32))
    return jnp.concatenate(pieces, 0)


def with_sum_row(values):
    lanes = values.shape[1]
    return jnp.concatenate(
        [values, jnp.ones((1, lanes), F32), jnp.zeros((7, lanes), F32)], 0
    ).astype(BF16)


def weights_of(scores, highest, depth):
    return jnp.exp2((scores - highest) * (math.log2(math.e) / math.sqrt(depth))).astype(BF16)


def ahead_of(items, score, finish, ahead):
    waiting = [score(item) for item in items[:ahead]]
    for k, item in enumerate(items):
        if k + ahead < len(items):
            waiting.append(score(items[k + ahead]))
        finish(item, *waiting.pop(0))


def attended(mixed, depth):
    return mixed[:depth] / mixed[depth : depth + 1]


def col_attention_kernel(depth, arrived, result, done, sems):
    count, lines, length = arrived.shape
    per = lines // (3 * depth)
    total = per * depth
    lanes = jnp.concatenate([arrived[s].astype(F32) for s in range(count)], 1)
    rest = lanes[total : 2 * total] * (math.log2(math.e) / math.sqrt(depth))
    key_rows = []
    for _ in range(3):
        key_rows.append(rest.astype(BF16).astype(F32))
        rest = rest - key_rows[-1]
    key_rows = jnp.concatenate(key_rows, 0).T.astype(BF16)
    values = [
        with_sum_row(lanes[2 * total + h * depth : 2 * total + (h + 1) * depth]) for h in range(per)
    ]
    block = 2 * length
    copies = [pltpu.make_async_copy(done.at[k], result.at[k], sems.at[k]) for k in range(count)]
    heads = []

    def score(item):
        begin, h = item
        queries = padded_rows(lanes[h * depth : (h + 1) * depth, begin : begin + block], h * depth, total)
        scores = dot(key_rows, jnp.concatenate([queries] * 3, 0).astype(BF16))
        return scores, jnp.max(scores, 0, keepdims=True)

    def finish(item, scores, highest):
        begin, h = item
        probs = jnp.exp2(scores - highest).astype(BF16)
        heads.append(attended(dot(values[h], probs), depth))
        if h == per - 1:
            both = jnp.concatenate(heads, 0).astype(BF16)
            heads.clear()
            for k in range(begin // length, (begin + block) // length):
                done[k] = both[:, k * length - begin : (k + 1) * length - begin]
                copies[k].start()

    ahead_of([(begin, h) for begin in range(0, count * length, block) for h in range(per)], score, finish, 6)
    for copy in copies:
        copy.wait()


def row_attention_kernel(count, queries, *refs):
    pairs = refs[:count]
    tokens, weight, bias, partial = refs[count:]
    stripes, half, length = queries.shape
    depth = half // HALF
    together = 2
    both, key_rows, lines, done = [], [], [], {}
    for a in range(stripes):
        both.append(jnp.concatenate([ref[a].astype(F32) for ref in pairs], 1))
        key_rows.append(both[a][:half].T.astype(BF16))
        lines.append(queries[a].astype(F32))

    def score(item):
        a, h = item
        wide = [
            padded_rows(lines[a][g * depth : (g + 1) * depth], g * depth, half)
            for g in range(h, h + together)
        ]
        scores = dot(key_rows[a], jnp.concatenate(wide, 1).astype(BF16))
        return scores, jnp.max(scores, 0, keepdims=True)

    def finish(item, scores, highest):
        a, h = item
        probs = weights_of(scores, highest, depth)
        for k in range(together):
            g = h + k
            values = with_sum_row(both[a][half + g * depth : half + (g + 1) * depth])
            done[a, g] = attended(dot(values, probs[:, k * length : (k + 1) * length]), depth)

    items = [(a, h) for a in range(stripes) for h in range(0, HALF, together)]
    ahead_of(items, score, finish, 2)
    for a in range(stripes):
        attention = jnp.concatenate([done[a, g] for g in range(HALF)], 0).T.astype(BF16)
        here = pl.ds(a * length, length)
        partial[here] = (
            tokens[here].astype(F32) + dot(attention, weight[:half]) + bias[...].reshape(1, 2 * half)
        )


def output_kernel(arrived, partial, weight, output):
    rows, cols, width = output.shape
    half = width // 2
    count = arrived.shape[0]
    across = cols // SPLIT
    down = rows // SPLIT
    square = SPLIT * SPLIT
    each = count // across
    blocks = {}
    for b in range(across):
        lines = jnp.concatenate([arrived[b * each + k].astype(F32) for k in range(each)], 0)
        mixed = dot(lines.T.astype(BF16), weight[half:])
        for a in range(down):
            here = pl.ds((a * across + b) * square, square)
            blocks[a, b] = (partial[here] + mixed[a * square : (a + 1) * square]).reshape(
                SPLIT, SPLIT, width
            )
    for a in range(down):
        output[a * SPLIT : (a + 1) * SPLIT] = jnp.concatenate(
            [blocks[a, b] for b in range(across)], 1
        ).astype(BF16)


def call(kernel, name, out_shape, args, flops, scratch=(), loose=()):
    several = isinstance(out_shape, tuple)
    spaces = [pl.ANY if k in loose else pltpu.VMEM for k in range(len(out_shape) if several else 1)]
    specs = tuple(pl.BlockSpec(memory_space=space) for space in spaces)
    moved = sum(x.size * x.dtype.itemsize for x in args)
    return pl.pallas_call(
        kernel,
        out_shape=out_shape,
        in_specs=vmem(len(args)),
        out_specs=specs if several else specs[0],
        scratch_shapes=scratch,
        compiler_params=params(),
        cost_estimate=pl.CostEstimate(flops=flops, bytes_accessed=moved, transcendentals=0),
        name=name,
    )(*args)


def shape(dims, dtype=BF16):
    return jax.ShapeDtypeStruct(dims, dtype)


def gathered(value, axis):
    count = lax.axis_size(axis)
    held = [value]
    for step in range(count - 1, 0, -1):
        pairs = [(k, k ^ step) for k in range(count)]
        held.append(lax.ppermute(value, axis, pairs))
    return held


def exchanged(value, axis):
    count = lax.axis_size(axis)
    lead = count // 4
    order = [lead] + [k for k in range(count) if k != lead]
    return lax.all_to_all(value, axis, 0, 0, axis_index_groups=[order], tiled=True)


def on_device(
    image,
    conv_weight,
    conv_bias,
    merge_gain,
    merge_shift,
    norm_gain,
    norm_shift,
    qkv_weight,
    proj_weight,
    proj_bias,
):
    in_rows, in_cols, channels = image.shape
    rows, cols = in_rows // 2, in_cols // 2
    width = conv_weight.shape[3]
    half = width // 2
    depth = width // HEADS
    row_count = lax.axis_size("row")
    col_count = lax.axis_size("col")
    down = [(k, (k + 1) % row_count) for k in range(row_count)]
    right = [(k, (k + 1) % col_count) for k in range(col_count)]
    diagonal = []
    for r in range(row_count):
        for c in range(col_count):
            target = (r, 0) if c == col_count - 1 else ((r + 1) % row_count, c + 1)
            diagonal.append((r * col_count + c, target[0] * col_count + target[1]))
    bottom = image[in_rows - 1]
    near = 2 * SPLIT
    tail = call(corner_kernel, "corner", shape((near, channels)), (bottom,), 10**10)
    side = call(edge_kernel, "edge", shape((in_rows, channels)), (image,), 10**5)
    upper = lax.ppermute(bottom, "row", down)
    left = lax.ppermute(side, "col", right)
    corner = lax.ppermute(tail, ("row", "col"), diagonal)
    pixel_parts = -(-channels // LANES)
    merged = call(
        own_kernel,
        "own_tile",
        shape((rows * cols, width), F32),
        (image, conv_weight),
        10**9,
        [pltpu.VMEM((pixel_parts, in_rows + 1, in_cols + 2 * SPLIT, LANES), F32)],
    )
    stripes, across = rows // SPLIT, cols // SPLIT
    per = across * HALF // row_count
    lanes = rows * SPLIT
    tokens, normed, chunks = call(
        merge_kernel,
        "merge",
        (
            shape((rows * cols, width)),
            shape((rows * cols, width)),
            shape((row_count, 3 * per * depth, lanes)),
        ),
        (
            merged,
            upper,
            left,
            corner,
            conv_weight,
            qkv_weight,
            conv_bias,
            merge_gain,
            merge_shift,
            norm_gain,
            norm_shift,
        ),
        5 * 10**8,
        [
            pltpu.VMEM((pixel_parts, 2, max(in_rows, in_cols) + 2 * SPLIT, LANES), F32),
            pltpu.VMEM((row_count, 3 * per * depth, lanes), BF16),
            pltpu.SemaphoreType.DMA((row_count,)),
        ],
        (2,),
    )
    arrived = exchanged(chunks, "row")
    queries, pairs = call(
        row_qkv_kernel,
        "row_qkv",
        (shape((stripes, half, cols * SPLIT)), shape((stripes, width, cols * SPLIT))),
        (normed, qkv_weight),
        3 * 10**8,
    )
    held = gathered(pairs, "col")
    result = call(
        lambda *refs: col_attention_kernel(depth, *refs),
        "col_attention",
        shape((row_count, per * depth, lanes)),
        (arrived,),
        2 * 10**9,
        [pltpu.VMEM((row_count, per * depth, lanes), BF16), pltpu.SemaphoreType.DMA((row_count,))],
        (0,),
    )
    back = exchanged(result, "row")
    partial = call(
        lambda *refs: row_attention_kernel(len(held), *refs),
        "row_attention",
        shape((rows * cols, width), F32),
        (queries, *held, tokens, proj_weight, proj_bias),
        2 * 10**9,
    )
    return call(
        output_kernel,
        "output",
        shape((rows, cols, width)),
        (back, partial, proj_weight),
        10**8,
    )


def solution(mesh):
    return jax.shard_map(
        on_device,
        mesh=mesh,
        in_specs=(P("row", "col", None), P(), P(), P(), P(), P(), P(), P(), P(), P()),
        out_specs=P("row", "col", None),
        check_vma=False,
    )
```
